256 devices in a mesh: ctx: 64 (over y, z, core), head: 4 (over x).
Axes of the slice: x: 4, y: 4, z: 8, core: 2. Of those that a mesh axis runs over, the one named last changes fastest.
Arguments:
- queries: bfloat16 [32768, 2048], P('ctx', 'head'), may hold values from -8 to 8
- keys: bfloat16 [32768, 128], P('ctx'), may hold values from -8 to 8
- values: bfloat16 [32768, 128], P('ctx'), may hold values from -6 to 6
- out_grad: bfloat16 [32768, 2048], P('ctx', 'head'), may hold values from -6 to 6
- doc_start: int32 [32768], P('ctx'), may hold values from 0 to 32767, as said below
- block_seq: int32 [64], replicated, may hold values from 0 to 63, as said below
Outputs:
- query_grad: bfloat16 [32768, 2048], P('ctx', 'head')
- key_grad: bfloat16 [32768, 128], P(('ctx', 'head'))
- value_grad: bfloat16 [32768, 128], P(('ctx', 'head'))
The draws below stay inside these ranges and needn't reach their ends.
Inputs may be any that keep to these rules, and one draw needn't show every extreme that they name: Position d along ctx holds sequence block block_seq[d]; block_seq is a permutation that maps each aligned pair of positions 2k and 2k + 1 onto itself. doc_start of a stored row is the sequence position of the first token of that row's document, at most the row's own position; documents are runs of consecutive positions of at most 1024 tokens, and one document has exactly 1024 tokens.
All inputs are finite; a program needn't handle non-finite values.
Results may differ from the reference program's by a relative error of at most 0.015.
Values may be sent and summed in bfloat16 or wider, within the bound.
A program may use at most 64 MiB of HBM per device.

```python
import math
import jax
import jax.numpy as jnp
from jax import lax

HEAD_DIM = 128
QHEADS = 16
TOK_DEV = 512
TOKENS = 32768
DOC_MOST = 1024
N_CTX = 64


def pair_order(key):
    flips = jax.random.randint(jax.random.fold_in(key, 101), (N_CTX // 2,), 0, 2)
    return jnp.bitwise_xor(jnp.arange(N_CTX, dtype=jnp.int32), jnp.repeat(flips, 2).astype(jnp.int32))


def row_scale(key, low, high):
    return jnp.exp(jax.random.uniform(key, (TOKENS, 1), jnp.float32, math.log(low), math.log(high)))


def draw_block_seq(key, part):
    order = pair_order(key)
    return order.astype(jnp.int32)


def draw_doc_start(key, part):
    order = pair_order(key)
    key = jax.random.fold_in(key, 2)
    frame = DOC_MOST
    phase = jax.random.randint(jax.random.fold_in(key, 1), (), 0, frame)
    places = jnp.arange(TOKENS, dtype=jnp.int32)
    shifted = places - phase
    frame_of = jnp.floor_divide(shifted, frame)
    full_frames = (TOKENS - phase) // frame
    chosen = jax.random.randint(jax.random.fold_in(key, 2), (), 0, full_frames - 1)
    coins = jax.random.randint(jax.random.fold_in(key, 3), (TOKENS,), 0, frame)
    starts = (jnp.remainder(shifted, frame) == 0) | (places == 0) | (places == TOKENS - 1) | (coins < 2) & (frame_of != chosen)
    begins = lax.cummax(jnp.where(starts, places, 0), axis=0)
    stored_pos = order[places // TOK_DEV] * TOK_DEV + places % TOK_DEV
    return begins[stored_pos].astype(jnp.int32)


def draw_queries(key, part):
    key = jax.random.fold_in(key, 3)
    result = jax.random.normal(key, (TOKENS, QHEADS * HEAD_DIM), jnp.float32) * row_scale(jax.random.fold_in(key, 1), 0.5, 2.5)
    return jnp.clip(result, -8.0, 8.0).astype(jnp.bfloat16)


def draw_keys(key, part):
    key = jax.random.fold_in(key, 4)
    result = jax.random.normal(key, (TOKENS, HEAD_DIM), jnp.float32) * row_scale(jax.random.fold_in(key, 1), 0.5, 2.5)
    return jnp.clip(result, -8.0, 8.0).astype(jnp.bfloat16)


def steps_of(stream_key, dims, pieces, smallest, high):
    level = 1.0
    for axis_at, blocks in pieces:
        heights = jax.random.uniform(jax.random.fold_in(jax.random.fold_in(stream_key, 6), axis_at), (blocks,), jnp.float32, smallest / len(pieces), high / len(pieces))
        level = level * jnp.repeat(jnp.exp(heights), dims[axis_at] // blocks).reshape((-1,) + (1,) * (len(dims) - 1 - axis_at))
    return level


def normal_values(rng, extent, scale, limit, split=(), held_as=jnp.bfloat16):
    loudness = steps_of(rng, extent, split, -0.22, 0.18) if split else 1.0
    values = jax.random.normal(rng, extent, jnp.float32) * scale * loudness
    return jnp.minimum(jnp.maximum(values, -limit), limit).astype(held_as)


def setup_inputs(seed: int = 0) -> dict:
    key_list = jax.random.split(jax.random.key(seed), 7)
    return {
        "queries": draw_queries(jax.random.fold_in(key_list[6], 71), 0),
        "keys": draw_keys(jax.random.fold_in(key_list[6], 71), 0),
        "values": normal_values(key_list[2], (TOKENS, HEAD_DIM), 1.0, 6.0, ((0, 64),)),
        "out_grad": normal_values(key_list[3], (TOKENS, QHEADS * HEAD_DIM), 1.0, 6.0, ((0, 64), (1, 4))),
        "doc_start": draw_doc_start(jax.random.fold_in(key_list[6], 71), 0),
        "block_seq": draw_block_seq(jax.random.fold_in(key_list[6], 71), 0),
    }


def reference(queries, keys, values, out_grad, doc_start, block_seq):
    score_scale = HEAD_DIM ** -0.5
    block_index = jnp.arange(N_CTX, dtype=jnp.int32)
    row_offsets = jnp.arange(TOK_DEV, dtype=jnp.int32)

    def locate(target):
        return jnp.sum(jnp.where(block_seq == target, block_index, 0)).astype(jnp.int32)

    def one_block(totals, stored):
        key_total, value_total = totals
        seq_block = jnp.sum(jnp.where(block_index == stored, block_seq, 0)).astype(jnp.int32)
        first_row = (stored * TOK_DEV).astype(jnp.int32)
        query_rows = lax.dynamic_slice_in_dim(queries, first_row, TOK_DEV, 0).astype(jnp.float32).reshape(TOK_DEV, QHEADS, HEAD_DIM)
        grad_rows = lax.dynamic_slice_in_dim(out_grad, first_row, TOK_DEV, 0).astype(jnp.float32).reshape(TOK_DEV, QHEADS, HEAD_DIM)
        start_rows = lax.dynamic_slice_in_dim(doc_start, first_row, TOK_DEV, 0)
        query_pos = seq_block * TOK_DEV + row_offsets
        holders = [locate(seq_block - back_step) for back_step in range(3)]
        key_pos = jnp.concatenate([(seq_block - back_step) * TOK_DEV + row_offsets for back_step in range(3)])
        key_rows = jnp.concatenate([lax.dynamic_slice_in_dim(keys, (holder * TOK_DEV).astype(jnp.int32), TOK_DEV, 0) for holder in holders]).astype(jnp.float32)
        value_rows = jnp.concatenate([lax.dynamic_slice_in_dim(values, (holder * TOK_DEV).astype(jnp.int32), TOK_DEV, 0) for holder in holders]).astype(jnp.float32)
        lower_bound = jnp.clip(start_rows, jnp.maximum(query_pos - DOC_MOST + 1, 0), query_pos)
        visible = (key_pos[None, :] <= query_pos[:, None]) & (key_pos[None, :] >= lower_bound[:, None])
        score = jnp.einsum("thd,kd->htk", query_rows, key_rows) * score_scale
        row_top = jnp.max(jnp.where(visible, score, -jnp.inf), axis=2, keepdims=True)
        weight = jnp.exp(jnp.where(visible, score - row_top, -jnp.inf))
        probability = weight / jnp.sum(weight, axis=2, keepdims=True)
        prob_grad = jnp.einsum("thd,kd->htk", grad_rows, value_rows)
        row_delta = jnp.sum(probability * prob_grad, axis=2, keepdims=True)
        score_grad = probability * (prob_grad - row_delta)
        prob_round = lax.optimization_barrier(probability.astype(jnp.bfloat16)).astype(jnp.float32)
        score_round = lax.optimization_barrier(score_grad.astype(jnp.bfloat16)).astype(jnp.float32)
        query_grad = (jnp.einsum("htk,kd->thd", score_round, key_rows) * score_scale).astype(jnp.bfloat16).reshape(TOK_DEV, QHEADS * HEAD_DIM)
        key_tiles = jnp.einsum("htk,thd->kd", score_round, query_rows) * score_scale
        value_tiles = jnp.einsum("htk,thd->kd", prob_round, grad_rows)
        for back_step in range(3):
            target_row = (holders[back_step] * TOK_DEV).astype(jnp.int32)
            key_piece = key_tiles[back_step * TOK_DEV:(back_step + 1) * TOK_DEV]
            value_piece = value_tiles[back_step * TOK_DEV:(back_step + 1) * TOK_DEV]
            key_total = lax.dynamic_update_slice_in_dim(key_total, lax.dynamic_slice_in_dim(key_total, target_row, TOK_DEV, 0) + key_piece, target_row, 0)
            value_total = lax.dynamic_update_slice_in_dim(value_total, lax.dynamic_slice_in_dim(value_total, target_row, TOK_DEV, 0) + value_piece, target_row, 0)
        return (key_total, value_total), query_grad

    empty_sum = jnp.zeros((N_CTX * TOK_DEV, HEAD_DIM), jnp.float32)
    (key_total, value_total), query_grad = lax.scan(one_block, (empty_sum, empty_sum), block_index)
    return query_grad.reshape(N_CTX * TOK_DEV, QHEADS * HEAD_DIM), key_total.astype(jnp.bfloat16), value_total.astype(jnp.bfloat16)
```

```python
import functools
import math

import jax
import jax.numpy as jnp
from jax import lax
from jax.experimental import pallas as pl
from jax.experimental.pallas import tpu as pltpu
from jax.sharding import PartitionSpec as P

MESH = pl.DeviceIdType.MESH
ROWS = 512
WIDTH = 128
HEADS = 4
QT = 128
KT = 256
COLS = HEADS * QT
MASKED = -1e30
VMEM_LIMIT = 56 * 1024 * 1024


def copy_to(src, dst, send, recv, ctx, head):
    return pltpu.make_async_remote_copy(
        src_ref=src,
        dst_ref=dst,
        send_sem=send,
        recv_sem=recv,
        device_id=(ctx, head),
        device_id_type=MESH,
    )


def greet(senders, count):
    barrier = pltpu.get_barrier_semaphore()
    for ctx, head in senders:
        pl.semaphore_signal(barrier, inc=1, device_id=(ctx, head), device_id_type=MESH)
    pl.semaphore_wait(barrier, count)


def fetch_kernel(n_ctx, k_ref, v_ref, kv_ref, send_z, recv_z, send_f, recv_f, send_p, recv_p, local):
    me = lax.axis_index("ctx")
    head = lax.axis_index("head")
    core = lax.rem(me, 2)
    partner = me + 1 - 2 * core
    after = lax.rem(me + 2, n_ctx)
    before = lax.rem(me + n_ctx - 2, n_ctx)
    greet([(partner, head), (before, head), (after, head)], 3)
    half = ROWS // 2
    parts = [(j, r) for r in range(2) for j in range(2)]
    refs = (k_ref, v_ref)
    out = []
    for i, (j, r) in enumerate(parts):
        rows = pl.ds(r * half, half)
        cp = copy_to(refs[j].at[rows], kv_ref.at[2 + core, j, rows], send_z.at[i], recv_z.at[i], after, head)
        cp.start()
        out.append(cp)
    near = []
    own = []
    for j in range(2):
        cp = copy_to(refs[j], kv_ref.at[1, j], send_p.at[j], recv_p.at[j], partner, head)
        cp.start()
        near.append(cp)
        cp = pltpu.make_async_copy(refs[j], kv_ref.at[0, j], local.at[j])
        cp.start()
        own.append(cp)
    forwards = []
    for i, (j, r) in enumerate(parts):
        rows = pl.ds(r * half, half)
        out[i].wait_recv()
        cp = copy_to(
            kv_ref.at[2 + core, j, rows], kv_ref.at[2 + core, j, rows], send_f.at[i], recv_f.at[i], partner, head
        )
        cp.start()
        forwards.append(cp)
    for cp in own + near + forwards:
        cp.wait()
    for cp in out:
        cp.wait_send()


def fetch(keys, values, n_ctx):
    return pl.pallas_call(
        functools.partial(fetch_kernel, n_ctx),
        out_shape=jax.ShapeDtypeStruct((4, 2, ROWS, WIDTH), jnp.bfloat16),
        in_specs=[pl.BlockSpec(memory_space=pl.ANY)] * 2,
        out_specs=pl.BlockSpec(memory_space=pl.ANY),
        scratch_shapes=[pltpu.SemaphoreType.DMA((4,))] * 4 + [pltpu.SemaphoreType.DMA((2,))] * 3,
        compiler_params=pltpu.CompilerParams(collective_id=0, has_side_effects=True),
        name="fetch",
    )(keys, values)


def dot(a, b, ca, cb):
    return lax.dot_general(a, b, (((ca,), (cb,)), ((), ())), preferred_element_type=jnp.float32)


def attend_kernel(
    n_ctx,
    pos_ref,
    seq_ref,
    start_ref,
    lower_ref,
    q_ref,
    do_ref,
    kv_ref,
    dq_ref,
    own_ref,
    near_ref,
    prev_ref,
    acc,
    p_scr,
    dp_scr,
    m_scr,
):
    me = pos_ref[0]
    tile = pl.program_id(0)
    core = lax.rem(me, 2)
    chip_before = lax.rem(me - core + n_ctx - 2, n_ctx)
    own = seq_ref[me]
    odd = lax.rem(own, 2) == 1
    slot1 = jnp.where(odd, 1, jnp.where(seq_ref[chip_before] == own - 1, 2, 3))
    slot2 = jnp.where(seq_ref[chip_before] == own - 2, 2, 3)
    base = (own - 2) * ROWS
    scale = WIDTH ** (-0.5)
    scale2 = scale * math.log2(math.e)

    @pl.when(tile == 0)
    def _():
        acc[...] = jnp.zeros_like(acc)

    first_row = 2 * ROWS + tile * QT
    row_pos = first_row + lax.broadcasted_iota(jnp.int32, (1, QT), 1)
    lower = jnp.clip(lower_ref[pl.ds(tile, 1), :] - base, jnp.maximum(row_pos - 2 * ROWS + 1, -base), row_pos)
    lo = jnp.clip(start_ref[tile * QT] - base, jnp.maximum(first_row - 2 * ROWS + 1, -base), first_row)
    lo_tile = lo // KT
    hi_tile = (first_row + QT - 1) // KT + 1

    q = jnp.concatenate([q_ref[:, h * WIDTH : (h + 1) * WIDTH] for h in range(HEADS)], axis=0)
    do = jnp.concatenate([do_ref[:, h * WIDTH : (h + 1) * WIDTH] for h in range(HEADS)], axis=0)

    def kv_tile(kt, which):
        role = kt // 2
        slot = jnp.where(role == 2, 0, jnp.where(role == 1, slot1, slot2))
        return kv_ref[slot, which, pl.ds((kt % 2) * KT, KT), :]

    def first_pass(kt, carry):
        m, l, d = carry
        k = kv_tile(kt, 0)
        v = kv_tile(kt, 1)
        key_pos = kt * KT + lax.broadcasted_iota(jnp.int32, (KT, QT), 0)
        bias = jnp.where((key_pos >= lower) & (key_pos <= row_pos), 0.0, MASKED)
        s = dot(k, q, 1, 1)
        dp = dot(v, do, 1, 1)
        s = s * scale2 + jnp.concatenate([bias] * HEADS, axis=1)
        m_new = jnp.maximum(m, jnp.max(s, axis=0, keepdims=True))
        p = jnp.exp2(s - m_new)
        shrink = jnp.exp2(m - m_new)
        l = l * shrink + jnp.sum(p, axis=0, keepdims=True)
        d = d * shrink + jnp.sum(p * dp, axis=0, keepdims=True)
        p_scr[kt] = p
        dp_scr[kt] = dp
        m_scr[kt] = m_new
        return m_new, l, d

    zero = jnp.zeros((1, COLS), jnp.float32)
    m, l, d = lax.fori_loop(lo_tile, hi_tile, first_pass, (zero + MASKED, zero, zero))
    inv = 1.0 / l
    delta = d * inv

    def second_pass(kt, dq):
        k = kv_tile(kt, 0)
        factor = jnp.exp2(m_scr[kt] - m) * inv
        p = p_scr[kt] * factor
        ds = (p * (dp_scr[kt] - delta)).astype(jnp.bfloat16)
        pb = p.astype(jnp.bfloat16)
        rows = pl.ds(kt * KT, KT)
        acc[rows, 0:WIDTH] += dot(ds, q, 1, 0)
        acc[rows, WIDTH : 2 * WIDTH] += dot(pb, do, 1, 0)
        return dq + dot(k, ds, 0, 0)

    dq = lax.fori_loop(lo_tile, hi_tile, second_pass, jnp.zeros((WIDTH, COLS), jnp.float32))
    for h in range(HEADS):
        piece = dq[:, h * QT : (h + 1) * QT] * scale
        dq_ref[:, h * WIDTH : (h + 1) * WIDTH] = piece.T.astype(dq_ref.dtype)

    @pl.when(tile == pl.num_programs(0) - 1)
    def _():
        def grads(role):
            g = acc[role * ROWS : (role + 1) * ROWS, :]
            return jnp.concatenate([g[:, :WIDTH] * scale, g[:, WIDTH:]], axis=1)

        own_ref[...] = grads(2)
        g1 = grads(1).astype(jnp.bfloat16)
        g2 = grads(0).astype(jnp.bfloat16)
        none = jnp.zeros_like(g1)
        near_ref[...] = jnp.where(odd, g1, none)
        prev_ref[0] = jnp.where(slot1 == 2, g1, jnp.where(slot2 == 2, g2, none))
        prev_ref[1] = jnp.where(slot1 == 3, g1, jnp.where(slot2 == 3, g2, none))


def attend(queries, out_grad, doc_start, block_seq, kv, n_ctx, pos):
    steps = ROWS // QT
    smem = pl.BlockSpec(memory_space=pltpu.SMEM)
    whole = lambda shape: pl.BlockSpec(shape, lambda i: (0,) * len(shape))
    return pl.pallas_call(
        functools.partial(attend_kernel, n_ctx),
        grid=(steps,),
        out_shape=(
            jax.ShapeDtypeStruct(queries.shape, jnp.bfloat16),
            jax.ShapeDtypeStruct((ROWS, 2 * WIDTH), jnp.float32),
            jax.ShapeDtypeStruct((ROWS, 2 * WIDTH), jnp.bfloat16),
            jax.ShapeDtypeStruct((2, ROWS, 2 * WIDTH), jnp.bfloat16),
        ),
        in_specs=[
            smem,
            smem,
            smem,
            whole((steps, QT)),
            pl.BlockSpec((QT, HEADS * WIDTH), lambda i: (i, 0)),
            pl.BlockSpec((QT, HEADS * WIDTH), lambda i: (i, 0)),
            whole((4, 2, ROWS, WIDTH)),
        ],
        out_specs=(
            pl.BlockSpec((QT, HEADS * WIDTH), lambda i: (i, 0)),
            whole((ROWS, 2 * WIDTH)),
            whole((ROWS, 2 * WIDTH)),
            whole((2, ROWS, 2 * WIDTH)),
        ),
        scratch_shapes=[
            pltpu.VMEM((3 * ROWS, 2 * WIDTH), jnp.float32),
            pltpu.VMEM((3 * ROWS // KT, KT, COLS), jnp.float32),
            pltpu.VMEM((3 * ROWS // KT, KT, COLS), jnp.float32),
            pltpu.VMEM((3 * ROWS // KT, 1, COLS), jnp.float32),
        ],
        compiler_params=pltpu.CompilerParams(vmem_limit_bytes=VMEM_LIMIT),
        name="attend",
    )(pos, block_seq, doc_start, doc_start.reshape(steps, QT), queries, out_grad, kv)


def give_back_kernel(
    n_ctx,
    n_head,
    own_ref,
    near_ref,
    prev_ref,
    dk_ref,
    dv_ref,
    got_near,
    got_prev,
    own_sum,
    own_cast,
    prev_sum,
    got_x,
    got_z,
    send_p,
    recv_p,
    send_x,
    recv_x,
    send_z,
    recv_z,
):
    me = lax.axis_index("ctx")
    head = lax.axis_index("head")
    core = lax.rem(me, 2)
    partner = me + 1 - 2 * core
    after = lax.rem(me + 2, n_ctx)
    before = lax.rem(me + n_ctx - 2, n_ctx)
    others = [lax.rem(head + s, n_head) for s in range(1, n_head)]
    peers = [(partner, head)] + [(me, x) for x in others] + [(after, x) for x in [head] + others]
    greet(peers, len(peers))
    part = ROWS // n_head
    to_prev = copy_to(prev_ref.at[1 - core], got_prev, send_p.at[0], recv_p.at[0], partner, head)
    to_near = copy_to(near_ref, got_near, send_p.at[1], recv_p.at[1], partner, head)
    to_prev.start()
    to_near.start()
    copies = []
    to_prev.wait_recv()
    prev_sum[...] = (prev_ref[core].astype(jnp.float32) + got_prev[...].astype(jnp.float32)).astype(jnp.bfloat16)
    for s in range(n_head):
        x = lax.rem(head + s, n_head)
        cp = copy_to(prev_sum.at[pl.ds(x * part, part)], got_z.at[s], send_z.at[s], recv_z.at[s], before, x)
        cp.start()
        copies.append(cp)
    to_near.wait_recv()
    own_sum[...] = own_ref[...] + got_near[...].astype(jnp.float32)
    mine = own_sum[pl.ds(head * part, part), :]
    own_cast[...] = own_sum[...].astype(jnp.bfloat16)
    for s in range(1, n_head):
        x = lax.rem(head + s, n_head)
        cp = copy_to(own_cast.at[pl.ds(x * part, part)], got_x.at[s - 1], send_x.at[s - 1], recv_x.at[s - 1], me, x)
        cp.start()
        copies.append(cp)
    for cp in copies:
        cp.wait_recv()
    total = mine
    for s in range(n_head - 1):
        total = total + got_x[s].astype(jnp.float32)
    for s in range(n_head):
        total = total + got_z[s].astype(jnp.float32)
    dk_ref[...] = total[:, :WIDTH].astype(jnp.bfloat16)
    dv_ref[...] = total[:, WIDTH:].astype(jnp.bfloat16)
    for cp in [to_prev, to_near] + copies:
        cp.wait_send()


def give_back(own, near, prev, n_ctx, n_head):
    part = ROWS // n_head
    vmem = pl.BlockSpec(memory_space=pltpu.VMEM)
    bf16 = jnp.bfloat16
    return pl.pallas_call(
        functools.partial(give_back_kernel, n_ctx, n_head),
        out_shape=(jax.ShapeDtypeStruct((part, WIDTH), bf16),) * 2,
        in_specs=[vmem] * 3,
        out_specs=(vmem, vmem),
        scratch_shapes=[
            pltpu.VMEM((ROWS, 2 * WIDTH), bf16),
            pltpu.VMEM((ROWS, 2 * WIDTH), bf16),
            pltpu.VMEM((ROWS, 2 * WIDTH), jnp.float32),
            pltpu.VMEM((ROWS, 2 * WIDTH), bf16),
            pltpu.VMEM((ROWS, 2 * WIDTH), bf16),
            pltpu.VMEM((n_head - 1, part, 2 * WIDTH), bf16),
            pltpu.VMEM((n_head, part, 2 * WIDTH), bf16),
            pltpu.SemaphoreType.DMA((2,)),
            pltpu.SemaphoreType.DMA((2,)),
            pltpu.SemaphoreType.DMA((n_head - 1,)),
            pltpu.SemaphoreType.DMA((n_head - 1,)),
            pltpu.SemaphoreType.DMA((n_head,)),
            pltpu.SemaphoreType.DMA((n_head,)),
        ],
        compiler_params=pltpu.CompilerParams(
            collective_id=1, has_side_effects=True, vmem_limit_bytes=VMEM_LIMIT
        ),
        name="give_back",
    )(own, near, prev)


def shards(queries, keys, values, out_grad, doc_start, block_seq):
    n_ctx = lax.axis_size("ctx")
    n_head = lax.axis_size("head")
    pos = lax.axis_index("ctx").astype(jnp.int32).reshape(1)
    kv = fetch(keys, values, n_ctx)
    query_grad, own, near, prev = attend(queries, out_grad, doc_start, block_seq, kv, n_ctx, pos)
    key_grad, value_grad = give_back(own, near, prev, n_ctx, n_head)
    return query_grad, key_grad, value_grad


def solution(mesh):
    return jax.shard_map(
        shards,
        mesh=mesh,
        in_specs=(
            P("ctx", "head"),
            P("ctx", None),
            P("ctx", None),
            P("ctx", "head"),
            P("ctx"),
            P(),
        ),
        out_specs=(P("ctx", "head"), P(("ctx", "head"), None), P(("ctx", "head"), None)),
        check_vma=False,
    )
```

```python
import functools
import math

import jax
import jax.numpy as jnp
from jax import lax
from jax.experimental import pallas as pl
from jax.experimental.pallas import tpu as pltpu
from jax.sharding import PartitionSpec as P

MESH = pl.DeviceIdType.MESH

ROWS = 512
WIDTH = 128
HEADS = 4
QT = 128
TILES = ROWS // QT
COLS = HEADS * QT
MASKED = -1e30
HALVES = 2
HALF = ROWS // HALVES
VMEM_LIMIT = 60 * 1024 * 1024
SCALE = WIDTH ** (-0.5)
SCALE2 = SCALE * math.log2(math.e)


def dot(a, b, ca, cb):
    return lax.dot_general(a, b, (((ca,), (cb,)), ((), ())), preferred_element_type=jnp.float32)


def bias_of(lower_ref, base, t, role, first_key, n_keys):
    row_pos = 2 * ROWS + t * QT + lax.broadcasted_iota(jnp.int32, (1, QT), 1)
    lower = jnp.clip(lower_ref[pl.ds(t, 1), :] - base, jnp.maximum(row_pos - 2 * ROWS + 1, -base), row_pos)
    key_pos = (2 - role) * ROWS + first_key + lax.broadcasted_iota(jnp.int32, (n_keys, QT), 0)
    seen = key_pos >= lower
    if role == 0:
        seen = seen & (key_pos <= row_pos)
    return jnp.where(seen, 0.0, MASKED)


def pass_one(role, t, first_key, n_keys, k, v, q, do, lower_ref, base, p_scr, dp_scr, m_scr, l_scr, d_scr):
    bias = bias_of(lower_ref, base, t, role, first_key, n_keys)
    s = dot(k, q, 1, 1) * SCALE2 + jnp.concatenate([bias] * HEADS, axis=1)
    dp = dot(v, do, 1, 1)
    top = jnp.max(s, axis=0, keepdims=True)
    if role > 0:
        m_old = m_scr[role - 1, t]
        m = jnp.maximum(m_old, top)
        shrink = jnp.exp2(m_old - m)
    else:
        m = top
    p = jnp.exp2(s - m)
    l = jnp.sum(p, axis=0, keepdims=True)
    d = jnp.sum(p * dp, axis=0, keepdims=True)
    if role > 0:
        l = l + l_scr[t] * shrink
        d = d + d_scr[t] * shrink
    m_scr[role, t] = m
    l_scr[t] = l
    d_scr[t] = d
    rows = pl.ds(first_key, n_keys)
    p_scr[role, t, rows, :] = p
    dp_scr[role, t, rows, :] = dp


def pass_two(role, t, first_key, n_keys, k, q, do, p_scr, dp_scr, m_scr, l_scr, d_scr, dq_acc):
    inv = 1.0 / l_scr[t]
    delta = d_scr[t] * inv
    factor = jnp.exp2(m_scr[role, t] - m_scr[2, t]) * inv
    rows = pl.ds(first_key, n_keys)
    p = p_scr[role, t, rows, :] * factor
    ds = (p * (dp_scr[role, t, rows, :] - delta)).astype(jnp.bfloat16)
    pb = p.astype(jnp.bfloat16)
    dq = dot(k, ds, 0, 0)
    if role == 1:
        dq_acc[t] = dq
    else:
        dq_acc[t] += dq
    return dot(ds, q, 1, 0), dot(pb, do, 1, 0)


def copy_to(src, dst, send, recv, ctx, head):
    return pltpu.make_async_remote_copy(
        src_ref=src,
        dst_ref=dst,
        send_sem=send,
        recv_sem=recv,
        device_id=(ctx, head),
        device_id_type=MESH,
    )


def backward_kernel(
    n_ctx,
    n_head,
    seq_ref,
    lower_ref,
    q_hbm,
    k_hbm,
    v_hbm,
    do_hbm,
    dq_hbm,
    dk_ref,
    dv_ref,
    qs,
    dos,
    kv,
    role_k,
    role_v,
    acc,
    p_scr,
    dp_scr,
    m_scr,
    l_scr,
    d_scr,
    dq_acc,
    dq_out,
    g1_out,
    g1_in,
    prev_out,
    own_out,
    got_z,
    got_x,
    swap_out,
    swap_in,
    load_sem,
    own_sem,
    store_sem,
    send_k,
    recv_k,
    send_p,
    recv_p,
    send_f,
    recv_f,
    send_g,
    recv_g,
    send_z,
    recv_z,
    send_x,
    recv_x,
    send_s,
    recv_s,
):
    me = lax.axis_index("ctx")
    head = lax.axis_index("head")
    core = lax.rem(me, 2)
    partner = me + 1 - 2 * core
    after = lax.rem(me + 2, n_ctx)
    before = lax.rem(me + n_ctx - 2, n_ctx)
    others = [lax.rem(head + s, n_head) for s in range(1, n_head)]
    part = ROWS // n_head

    loads = []
    for which, src in ((0, k_hbm), (1, v_hbm)):
        cp = pltpu.make_async_copy(src, kv.at[0, which], own_sem.at[which])
        cp.start()
        loads.append(cp)
    for t in range(TILES):
        for h in range(HEADS):
            for i, (src, dst) in enumerate(((q_hbm, qs), (do_hbm, dos))):
                cp = pltpu.make_async_copy(
                    src.at[pl.ds(t * QT, QT), pl.ds(h * WIDTH, WIDTH)], dst.at[t, pl.ds(h * QT, QT)], load_sem.at[i, t, h]
                )
                cp.start()
                loads.append(cp)

    barrier = pltpu.get_barrier_semaphore()
    senders = [(partner, head), (before, head), (after, head)] + [(after, x) for x in others] + [(me, x) for x in others]
    for ctx, x in senders:
        pl.semaphore_signal(barrier, inc=1, device_id=(ctx, x), device_id_type=MESH)
    pl.semaphore_wait(barrier, len(senders))

    far = []
    for r in range(HALVES):
        for which, src in ((0, k_hbm), (1, v_hbm)):
            rows = pl.ds(r * HALF, HALF)
            i = 2 * r + which
            cp = copy_to(src.at[rows], kv.at[2 + core, which, rows], send_k.at[i], recv_k.at[i], after, head)
            cp.start()
            far.append(cp)
    near = []
    for which, src in ((0, k_hbm), (1, v_hbm)):
        cp = copy_to(src, kv.at[1, which], send_p.at[which], recv_p.at[which], partner, head)
        cp.start()
        near.append(cp)

    own = seq_ref[me]
    odd = lax.rem(own, 2) == 1
    core_is_first = seq_ref[before - core] == own - lax.rem(own, 2) - 2
    base = (own - 2) * ROWS
    stats = (p_scr, dp_scr, m_scr, l_scr, d_scr)
    for cp in loads:
        cp.wait()
    for t in range(TILES):
        n = (t + 1) * QT
        pass_one(0, t, 0, n, kv[0, 0, :n], kv[0, 1, :n], qs[t], dos[t], lower_ref, base, *stats)

    forwards = []
    for r in range(HALVES):
        for which in range(2):
            i = 2 * r + which
            rows = pl.ds(r * HALF, HALF)
            far[i].wait_recv()
            cp = copy_to(
                kv.at[2 + core, which, rows], kv.at[2 + core, which, rows], send_f.at[i], recv_f.at[i], partner, head
            )
            cp.start()
            forwards.append(cp)
    for cp in near + forwards:
        cp.wait_recv()
    for which, dst in ((0, role_k), (1, role_v)):
        even_rows = jnp.where(core_is_first, kv[2, which], kv[3, which])
        odd_rows = jnp.where(core_is_first, kv[3, which], kv[2, which])
        dst[0] = jnp.where(odd, kv[1, which], odd_rows)
        dst[1] = jnp.where(odd, odd_rows, even_rows)

    def one(t, _):
        pass_one(1, t, 0, ROWS, role_k[0], role_v[0], qs[t], dos[t], lower_ref, base, *stats)
        return 0

    lax.fori_loop(0, TILES, one, 0)
    for t in range(TILES):
        f = t * QT
        n = ROWS - f
        pass_one(2, t, f, n, role_k[1, f:], role_v[1, f:], qs[t], dos[t], lower_ref, base, *stats)
    acc[...] = jnp.zeros_like(acc)

    def grads(role):
        return jnp.concatenate([acc[role, :, :WIDTH] * SCALE, acc[role, :, WIDTH:]], axis=1)

    def two(t, _):
        dk, dv = pass_two(1, t, 0, ROWS, role_k[0], qs[t], dos[t], *stats, dq_acc)
        acc[1, :, :WIDTH] += dk
        acc[1, :, WIDTH:] += dv
        return 0

    lax.fori_loop(0, TILES, two, 0)
    g1_out[...] = grads(1).astype(jnp.bfloat16)
    trade = copy_to(g1_out, g1_in, send_g, recv_g, partner, head)
    trade.start()
    for t in range(TILES):
        f = t * QT
        n = ROWS - f
        dk, dv = pass_two(2, t, f, n, role_k[1, f:], qs[t], dos[t], *stats, dq_acc)
        acc[2, f:, :WIDTH] += dk
        acc[2, f:, WIDTH:] += dv
    trade.wait_recv()
    none = jnp.zeros((ROWS, 2 * WIDTH), jnp.float32)
    traded = g1_in[...].astype(jnp.float32)
    prev_out[...] = (grads(2) + jnp.where(odd, traded, none)).astype(jnp.bfloat16)
    back = []
    for s in range(n_head):
        x = lax.rem(head + s, n_head)
        cp = copy_to(prev_out.at[pl.ds(x * part, part)], got_z.at[s], send_z.at[s], recv_z.at[s], before, x)
        cp.start()
        back.append(cp)
    stores = []
    for t in range(TILES):
        n = (t + 1) * QT
        dk, dv = pass_two(0, t, 0, n, kv[0, 0, :n], qs[t], dos[t], *stats, dq_acc)
        acc[0, :n, :WIDTH] += dk
        acc[0, :n, WIDTH:] += dv
        rows = pl.ds(t * QT, QT)
        for h in range(HEADS):
            piece = dq_acc[t, :, h * QT : (h + 1) * QT] * SCALE
            dq_out[rows, h * WIDTH : (h + 1) * WIDTH] = piece.T.astype(dq_out.dtype)
        cp = pltpu.make_async_copy(dq_out.at[rows], dq_hbm.at[rows], store_sem.at[t])
        cp.start()
        stores.append(cp)
    acc[0] = grads(0) + jnp.where(odd, none, g1_in[...].astype(jnp.float32))
    own_out[...] = acc[0].astype(jnp.bfloat16)
    across = []
    for s in range(1, n_head):
        x = lax.rem(head + s, n_head)
        cp = copy_to(own_out.at[pl.ds(x * part, part)], got_x.at[s - 1], send_x.at[s - 1], recv_x.at[s - 1], me, x)
        cp.start()
        across.append(cp)
    for cp in back:
        cp.wait_recv()
    came = got_z[0].astype(jnp.float32)
    for s in range(1, n_head):
        came = came + got_z[s].astype(jnp.float32)
    swap_out[...] = came.astype(jnp.bfloat16)
    swap = copy_to(swap_out, swap_in, send_s, recv_s, partner, head)
    swap.start()
    total = acc[0, pl.ds(head * part, part), :]
    for cp in across:
        cp.wait_recv()
    for s in range(n_head - 1):
        total = total + got_x[s].astype(jnp.float32)
    swap.wait_recv()
    straight = lax.rem(seq_ref[after], 2) == lax.rem(own, 2)
    total = total + jnp.where(straight, came, swap_in[...].astype(jnp.float32))
    dk_ref[...] = total[:, :WIDTH].astype(jnp.bfloat16)
    dv_ref[...] = total[:, WIDTH:].astype(jnp.bfloat16)
    for cp in stores:
        cp.wait()
    for cp in far + near + forwards + [trade] + back + across + [swap]:
        cp.wait_send()


def shards(queries, keys, values, out_grad, doc_start, block_seq):
    n_ctx = lax.axis_size("ctx")
    n_head = lax.axis_size("head")
    part = ROWS // n_head
    smem = pl.BlockSpec(memory_space=pltpu.SMEM)
    vmem = pl.BlockSpec(memory_space=pltpu.VMEM)
    hbm = pl.BlockSpec(memory_space=pl.ANY)
    f32 = jnp.float32
    bf16 = jnp.bfloat16
    dma = pltpu.SemaphoreType.DMA
    return pl.pallas_call(
        functools.partial(backward_kernel, n_ctx, n_head),
        out_shape=(
            jax.ShapeDtypeStruct(queries.shape, bf16),
            jax.ShapeDtypeStruct((part, WIDTH), bf16),
            jax.ShapeDtypeStruct((part, WIDTH), bf16),
        ),
        in_specs=[smem, vmem, hbm, hbm, hbm, hbm],
        out_specs=(hbm, vmem, vmem),
        scratch_shapes=[
            pltpu.VMEM((TILES, COLS, WIDTH), bf16),
            pltpu.VMEM((TILES, COLS, WIDTH), bf16),
            pltpu.VMEM((4, 2, ROWS, WIDTH), bf16),
            pltpu.VMEM((2, ROWS, WIDTH), bf16),
            pltpu.VMEM((2, ROWS, WIDTH), bf16),
            pltpu.VMEM((3, ROWS, 2 * WIDTH), f32),
            pltpu.VMEM((3, TILES, ROWS, COLS), f32),
            pltpu.VMEM((3, TILES, ROWS, COLS), f32),
            pltpu.VMEM((3, TILES, 1, COLS), f32),
            pltpu.VMEM((TILES, 1, COLS), f32),
            pltpu.VMEM((TILES, 1, COLS), f32),
            pltpu.VMEM((TILES, WIDTH, COLS), f32),
            pltpu.VMEM((ROWS, HEADS * WIDTH), bf16),
            pltpu.VMEM((ROWS, 2 * WIDTH), bf16),
            pltpu.VMEM((ROWS, 2 * WIDTH), bf16),
            pltpu.VMEM((ROWS, 2 * WIDTH), bf16),
            pltpu.VMEM((ROWS, 2 * WIDTH), bf16),
            pltpu.VMEM((n_head, part, 2 * WIDTH), bf16),
            pltpu.VMEM((n_head - 1, part, 2 * WIDTH), bf16),
            pltpu.VMEM((part, 2 * WIDTH), bf16),
            pltpu.VMEM((part, 2 * WIDTH), bf16),
            dma((2, TILES, HEADS)),
            dma((2,)),
            dma((TILES,)),
            dma((4,)),
            dma((4,)),
            dma((2,)),
            dma((2,)),
            dma((4,)),
            dma((4,)),
            dma,
            dma,
            dma((n_head,)),
            dma((n_head,)),
            dma((n_head - 1,)),
            dma((n_head - 1,)),
            dma,
            dma,
        ],
        compiler_params=pltpu.CompilerParams(
            collective_id=0, has_side_effects=True, vmem_limit_bytes=VMEM_LIMIT
        ),
        name="backward",
    )(block_seq, doc_start.reshape(TILES, QT), queries, keys, values, out_grad)


def solution(mesh):
    return jax.shard_map(
        shards,
        mesh=mesh,
        in_specs=(
            P("ctx", "head"),
            P("ctx", None),
            P("ctx", None),
            P("ctx", "head"),
            P("ctx"),
            P(),
        ),
        out_specs=(P("ctx", "head"), P(("ctx", "head"), None), P(("ctx", "head"), None)),
        check_vma=False,
    )
```

```python
import functools
import math

import jax
import jax.numpy as jnp
from jax import lax
from jax.experimental import pallas as pl
from jax.experimental.pallas import tpu as pltpu
from jax.sharding import PartitionSpec as P

MESH = pl.DeviceIdType.MESH

ROWS = 512
WIDTH = 128
HEADS = 4
QT = 128
TILES = ROWS // QT
COLS = HEADS * QT
MASKED = -1e30
CHUNKS = TILES
VMEM_LIMIT = 59 * 1024 * 1024 + 512 * 1024
SCALE = WIDTH ** (-0.5)
SCALE2 = SCALE * math.log2(math.e)


def dot(a, b, ca, cb):
    return lax.dot_general(a, b, (((ca,), (cb,)), ((), ())), preferred_element_type=jnp.float32)


def update(step, t, k, v, q, do, key_pos, causal, lower_ref, base, p_dst, dp_dst, m_scr, l_scr, d_scr):
    row_pos = 2 * ROWS + t * QT + lax.broadcasted_iota(jnp.int32, (1, QT), 1)
    lower = jnp.clip(lower_ref[pl.ds(t, 1), :] - base, jnp.maximum(row_pos - 2 * ROWS + 1, -base), row_pos)
    seen = key_pos >= lower
    if causal:
        seen = seen & (key_pos <= row_pos)
    bias = jnp.where(seen, 0.0, MASKED)
    s = dot(k, q, 1, 1) * SCALE2 + jnp.concatenate([bias] * HEADS, axis=1)
    dp = dot(v, do, 1, 1)
    m = jnp.max(s, axis=0, keepdims=True)
    if step > 0:
        m_old = m_scr[step - 1, t]
        m = jnp.maximum(m_old, m)
        shrink = jnp.exp2(m_old - m)
    p = jnp.exp2(s - m)
    l = jnp.sum(p, axis=0, keepdims=True)
    d = jnp.sum(p * dp, axis=0, keepdims=True)
    if step > 0:
        l = l + l_scr[t] * shrink
        d = d + d_scr[t] * shrink
    m_scr[step, t] = m
    l_scr[t] = l
    d_scr[t] = d
    p_dst[...] = p
    dp_dst[...] = dp


def key_grads(p, dp, factor, delta, q, do, ds_dst):
    n = ds_dst.shape[0]
    p = (p * factor).reshape(n, COLS)
    ds = (p * (dp.reshape(n, COLS) - delta)).astype(jnp.bfloat16)
    ds_dst[...] = ds
    return dot(ds, q, 1, 0), dot(p.astype(jnp.bfloat16), do, 1, 0)


def copy_to(src, dst, send, recv, ctx, head):
    return pltpu.make_async_remote_copy(
        src_ref=src,
        dst_ref=dst,
        send_sem=send,
        recv_sem=recv,
        device_id=(ctx, head),
        device_id_type=MESH,
    )


def backward_kernel(
    n_ctx,
    n_head,
    seq_ref,
    lower_ref,
    q_hbm,
    k_hbm,
    v_hbm,
    do_hbm,
    dq_out,
    dk_ref,
    dv_ref,
    qs,
    dos,
    kv,
    role_k,
    role_v,
    acc,
    p_own,
    dp_own,
    p_far,
    dp_far,
    ds_0,
    ds_1,
    ds_2,
    m_scr,
    l_scr,
    d_scr,
    g1_out,
    g1_in,
    prev_out,
    own_out,
    got_z,
    got_x,
    swap_out,
    swap_in,
    load_sem,
    own_sem,
    send_k,
    recv_k,
    send_p,
    recv_p,
    send_f,
    recv_f,
    send_g,
    recv_g,
    send_z,
    recv_z,
    send_x,
    recv_x,
    send_s,
    recv_s,
):
    me = lax.axis_index("ctx")
    head = lax.axis_index("head")
    core = lax.rem(me, 2)
    partner = me + 1 - 2 * core
    after = lax.rem(me + 2, n_ctx)
    before = lax.rem(me + n_ctx - 2, n_ctx)
    others = [lax.rem(head + s, n_head) for s in range(1, n_head)]
    part = ROWS // n_head

    loads = []
    for which, src in ((0, k_hbm), (1, v_hbm)):
        cp = pltpu.make_async_copy(src, kv.at[0, which], own_sem.at[which])
        cp.start()
        loads.append(cp)
    for t in range(TILES):
        for h in range(HEADS):
            for i, (src, dst) in enumerate(((q_hbm, qs), (do_hbm, dos))):
                cp = pltpu.make_async_copy(
                    src.at[pl.ds(t * QT, QT), pl.ds(h * WIDTH, WIDTH)], dst.at[t, pl.ds(h * QT, QT)], load_sem.at[i, t, h]
                )
                cp.start()
                loads.append(cp)

    barrier = pltpu.get_barrier_semaphore()
    senders = [(partner, head), (before, head), (after, head)] + [(after, x) for x in others] + [(me, x) for x in others]
    for ctx, x in senders:
        pl.semaphore_signal(barrier, inc=1, device_id=(ctx, x), device_id_type=MESH)
    pl.semaphore_wait(barrier, len(senders))

    far = []
    for r in range(CHUNKS):
        for which, src in ((0, k_hbm), (1, v_hbm)):
            rows = pl.ds(r * QT, QT)
            i = 2 * r + which
            cp = copy_to(src.at[rows], kv.at[2 + core, which, rows], send_k.at[i], recv_k.at[i], after, head)
            cp.start()
            far.append(cp)
    near = []
    for which, src in ((0, k_hbm), (1, v_hbm)):
        cp = copy_to(src, kv.at[1, which], send_p.at[which], recv_p.at[which], partner, head)
        cp.start()
        near.append(cp)

    own = seq_ref[me]
    odd = lax.rem(own, 2) == 1
    core_is_first = seq_ref[before - core] == own - lax.rem(own, 2) - 2
    base = (own - 2) * ROWS
    stats = (m_scr, l_scr, d_scr)
    for cp in loads:
        cp.wait()
    for t in range(TILES):
        n = (t + 1) * QT
        key_pos = 2 * ROWS + lax.broadcasted_iota(jnp.int32, (n, QT), 0)
        update(
            0, t, kv[0, 0, :n], kv[0, 1, :n], qs[t], dos[t], key_pos, True, lower_ref, base,
            p_own.at[t, pl.ds(0, n)], dp_own.at[t, pl.ds(0, n)], *stats,
        )

    forwards = []

    def pass_on(r):
        rows = pl.ds(r * QT, QT)
        for which in range(2):
            i = 2 * r + which
            far[i].wait_recv()
            place = kv.at[2 + core, which, rows]
            cp = copy_to(place, place, send_f.at[i], recv_f.at[i], partner, head)
            cp.start()
            forwards.append(cp)

    pass_on(0)
    for cp in near:
        cp.wait_recv()
    for r in range(CHUNKS):
        if r + 1 < CHUNKS:
            pass_on(r + 1)
        rows = slice(r * QT, (r + 1) * QT)
        for which, dst in ((0, role_k), (1, role_v)):
            forwards[2 * r + which].wait_recv()
            even_rows = jnp.where(core_is_first, kv[2, which, rows], kv[3, which, rows])
            odd_rows = jnp.where(core_is_first, kv[3, which, rows], kv[2, which, rows])
            dst[r, :QT] = jnp.where(odd, kv[1, which, rows], odd_rows)
            dst[r, QT:] = jnp.where(odd, odd_rows, even_rows)
        for t in range(TILES):
            n = 2 * QT if t <= r else QT
            row = lax.broadcasted_iota(jnp.int32, (n, QT), 0)
            key_pos = r * QT + row + jnp.where(row < QT, ROWS, -QT)
            update(
                r + 1, t, role_k[r, :n], role_v[r, :n], qs[t], dos[t], key_pos, False, lower_ref, base,
                p_far.at[r, t, pl.ds(0, n)], dp_far.at[r, t, pl.ds(0, n)], *stats,
            )

    for t in range(TILES):
        inv = 1.0 / l_scr[t]
        l_scr[t] = inv
        d_scr[t] = d_scr[t] * inv
    for t in range(TILES):
        factor = jnp.exp2(m_scr[1:, t] - m_scr[CHUNKS, t][None]) * l_scr[t][None]
        dk, dv = key_grads(p_far[:, t, :QT], dp_far[:, t, :QT], factor, d_scr[t], qs[t], dos[t], ds_1.at[t])
        if t == 0:
            acc[1, :, :WIDTH] = dk
            acc[1, :, WIDTH:] = dv
        else:
            acc[1, :, :WIDTH] += dk
            acc[1, :, WIDTH:] += dv

    def grads(role):
        return jnp.concatenate([acc[role, :, :WIDTH] * SCALE, acc[role, :, WIDTH:]], axis=1)

    g1_out[...] = grads(1).astype(jnp.bfloat16)
    trade = copy_to(g1_out, g1_in, send_g, recv_g, partner, head)
    trade.start()
    for t in range(TILES):
        f = t * QT
        factor = jnp.exp2(m_scr[1 + t :, t] - m_scr[CHUNKS, t][None]) * l_scr[t][None]
        dk, dv = key_grads(
            p_far[t:, t, QT:], dp_far[t:, t, QT:], factor, d_scr[t], qs[t], dos[t], ds_2.at[t, pl.ds(f, ROWS - f)]
        )
        if t == 0:
            acc[2, :, :WIDTH] = dk
            acc[2, :, WIDTH:] = dv
        else:
            acc[2, f:, :WIDTH] += dk
            acc[2, f:, WIDTH:] += dv
    trade.wait_recv()
    none = jnp.zeros((ROWS, 2 * WIDTH), jnp.float32)
    traded = g1_in[...].astype(jnp.float32)
    prev_out[...] = (grads(2) + jnp.where(odd, traded, none)).astype(jnp.bfloat16)
    back = []
    for s in range(n_head):
        x = lax.rem(head + s, n_head)
        cp = copy_to(prev_out.at[pl.ds(x * part, part)], got_z.at[s], send_z.at[s], recv_z.at[s], before, x)
        cp.start()
        back.append(cp)
    for t in reversed(range(TILES)):
        n = (t + 1) * QT
        factor = jnp.exp2(m_scr[0, t] - m_scr[CHUNKS, t]) * l_scr[t]
        dk, dv = key_grads(
            p_own[t, :n], dp_own[t, :n], factor, d_scr[t], qs[t], dos[t], ds_0.at[t, pl.ds(0, n)]
        )
        if t == TILES - 1:
            acc[0, :, :WIDTH] = dk
            acc[0, :, WIDTH:] = dv
        else:
            acc[0, :n, :WIDTH] += dk
            acc[0, :n, WIDTH:] += dv
    acc[0] = grads(0) + jnp.where(odd, none, g1_in[...].astype(jnp.float32))
    own_out[...] = acc[0].astype(jnp.bfloat16)
    across = []
    for s in range(1, n_head):
        x = lax.rem(head + s, n_head)
        cp = copy_to(own_out.at[pl.ds(x * part, part)], got_x.at[s - 1], send_x.at[s - 1], recv_x.at[s - 1], me, x)
        cp.start()
        across.append(cp)
    for t in range(TILES):
        n = (t + 1) * QT
        f = t * QT
        k1 = role_k[:, :QT].reshape(ROWS, WIDTH)
        k2 = role_k[t:, QT:].reshape(ROWS - f, WIDTH)
        dq = dot(kv[0, 0, :n], ds_0[t, :n], 0, 0) + dot(k1, ds_1[t], 0, 0) + dot(k2, ds_2[t, f:], 0, 0)
        dq = dq * SCALE
        rows = pl.ds(t * QT, QT)
        for h in range(HEADS):
            dq_out[rows, h * WIDTH : (h + 1) * WIDTH] = dq[:, h * QT : (h + 1) * QT].T.astype(dq_out.dtype)
    for cp in back:
        cp.wait_recv()
    came = got_z[0].astype(jnp.float32)
    for s in range(1, n_head):
        came = came + got_z[s].astype(jnp.float32)
    swap_out[...] = came.astype(jnp.bfloat16)
    swap = copy_to(swap_out, swap_in, send_s, recv_s, partner, head)
    swap.start()
    total = acc[0, pl.ds(head * part, part), :]
    for cp in across:
        cp.wait_recv()
    for s in range(n_head - 1):
        total = total + got_x[s].astype(jnp.float32)
    swap.wait_recv()
    straight = lax.rem(seq_ref[after], 2) == lax.rem(own, 2)
    total = total + jnp.where(straight, came, swap_in[...].astype(jnp.float32))
    dk_ref[...] = total[:, :WIDTH].astype(jnp.bfloat16)
    dv_ref[...] = total[:, WIDTH:].astype(jnp.bfloat16)
    for cp in far + near + forwards + [trade] + back + across + [swap]:
        cp.wait_send()


def hand_on_kernel(dq_ref, dk_ref, dv_ref, dq_out, dk_out, dv_out, sem):
    copies = []
    for i, (src, dst) in enumerate(((dq_ref, dq_out), (dk_ref, dk_out), (dv_ref, dv_out))):
        cp = pltpu.make_async_copy(src, dst, sem.at[i])
        cp.start()
        copies.append(cp)
    for cp in copies:
        cp.wait()


def shards(queries, keys, values, out_grad, doc_start, block_seq):
    n_ctx = lax.axis_size("ctx")
    n_head = lax.axis_size("head")
    part = ROWS // n_head
    smem = pl.BlockSpec(memory_space=pltpu.SMEM)
    vmem = pl.BlockSpec(memory_space=pltpu.VMEM)
    hbm = pl.BlockSpec(memory_space=pltpu.HBM)
    f32 = jnp.float32
    bf16 = jnp.bfloat16
    dma = pltpu.SemaphoreType.DMA
    grads = pl.pallas_call(
        functools.partial(backward_kernel, n_ctx, n_head),
        out_shape=(
            pltpu.VMEM(queries.shape, bf16),
            pltpu.VMEM((part, WIDTH), bf16),
            pltpu.VMEM((part, WIDTH), bf16),
        ),
        in_specs=[smem, vmem, hbm, hbm, hbm, hbm],
        out_specs=(vmem, vmem, vmem),
        scratch_shapes=[
            pltpu.VMEM((TILES, COLS, WIDTH), bf16),
            pltpu.VMEM((TILES, COLS, WIDTH), bf16),
            pltpu.VMEM((4, 2, ROWS, WIDTH), bf16),
            pltpu.VMEM((CHUNKS, 2 * QT, WIDTH), bf16),
            pltpu.VMEM((CHUNKS, 2 * QT, WIDTH), bf16),
            pltpu.VMEM((3, ROWS, 2 * WIDTH), f32),
            pltpu.VMEM((TILES, ROWS, COLS), f32),
            pltpu.VMEM((TILES, ROWS, COLS), f32),
            pltpu.VMEM((CHUNKS, TILES, 2 * QT, COLS), f32),
            pltpu.VMEM((CHUNKS, TILES, 2 * QT, COLS), f32),
            pltpu.VMEM((TILES, ROWS, COLS), bf16),
            pltpu.VMEM((TILES, ROWS, COLS), bf16),
            pltpu.VMEM((TILES, ROWS, COLS), bf16),
            pltpu.VMEM((CHUNKS + 1, TILES, 1, COLS), f32),
            pltpu.VMEM((TILES, 1, COLS), f32),
            pltpu.VMEM((TILES, 1, COLS), f32),
            pltpu.VMEM((ROWS, 2 * WIDTH), bf16),
            pltpu.VMEM((ROWS, 2 * WIDTH), bf16),
            pltpu.VMEM((ROWS, 2 * WIDTH), bf16),
            pltpu.VMEM((ROWS, 2 * WIDTH), bf16),
            pltpu.VMEM((n_head, part, 2 * WIDTH), bf16),
            pltpu.VMEM((n_head - 1, part, 2 * WIDTH), bf16),
            pltpu.VMEM((part, 2 * WIDTH), bf16),
            pltpu.VMEM((part, 2 * WIDTH), bf16),
            dma((2, TILES, HEADS)),
            dma((2,)),
            dma((2 * CHUNKS,)),
            dma((2 * CHUNKS,)),
            dma((2,)),
            dma((2,)),
            dma((2 * CHUNKS,)),
            dma((2 * CHUNKS,)),
            dma,
            dma,
            dma((n_head,)),
            dma((n_head,)),
            dma((n_head - 1,)),
            dma((n_head - 1,)),
            dma,
            dma,
        ],
        compiler_params=pltpu.CompilerParams(
            collective_id=0, has_side_effects=True, vmem_limit_bytes=VMEM_LIMIT
        ),
        name="backward",
    )(block_seq, doc_start.reshape(TILES, QT), queries, keys, values, out_grad)
    return pl.pallas_call(
        hand_on_kernel,
        out_shape=tuple(jax.ShapeDtypeStruct(g.shape, g.dtype) for g in grads),
        in_specs=[vmem] * 3,
        out_specs=(hbm,) * 3,
        scratch_shapes=[dma((3,))],
        compiler_params=pltpu.CompilerParams(vmem_limit_bytes=1024 * 1024),
        name="hand_on",
    )(*grads)


def solution(mesh):
    return jax.shard_map(
        shards,
        mesh=mesh,
        in_specs=(
            P("ctx", "head"),
            P("ctx", None),
            P("ctx", None),
            P("ctx", "head"),
            P("ctx"),
            P(),
        ),
        out_specs=(P("ctx", "head"), P(("ctx", "head"), None), P(("ctx", "head"), None)),
        check_vma=False,
    )
```

```python
import functools
import math

import jax
import jax.numpy as jnp
from jax import lax
from jax.experimental import pallas as pl
from jax.experimental.pallas import tpu as pltpu
from jax.sharding import PartitionSpec as P

MESH = pl.DeviceIdType.MESH

ROWS = 512
WIDTH = 128
HEADS = 4
QT = 128
TILES = ROWS // QT
COLS = HEADS * QT
MASKED = -1e30
CHUNKS = TILES
STRAIGHT = 80
VMEM_LIMIT = 59 * 1024 * 1024 + 512 * 1024
SCALE = WIDTH ** (-0.5)
SCALE2 = SCALE * math.log2(math.e)


def dot(a, b, ca, cb):
    return lax.dot_general(a, b, (((ca,), (cb,)), ((), ())), preferred_element_type=jnp.float32)


def update(step, t, k, v, q, do, key_pos, causal, lower_ref, base, p_dst, dp_dst, m_scr, l_scr, d_scr):
    row_pos = 2 * ROWS + t * QT + lax.broadcasted_iota(jnp.int32, (1, QT), 1)
    lower = jnp.clip(lower_ref[pl.ds(t, 1), :] - base, jnp.maximum(row_pos - 2 * ROWS + 1, -base), row_pos)
    seen = key_pos >= lower
    if causal:
        seen = seen & (key_pos <= row_pos)
    bias = jnp.where(seen, 0.0, MASKED)
    s = dot(k, q, 1, 1) * SCALE2 + jnp.concatenate([bias] * HEADS, axis=1)
    dp = dot(v, do, 1, 1)
    m = jnp.max(s, axis=0, keepdims=True)
    if step > 0:
        m_old = m_scr[step - 1, t]
        m = jnp.maximum(m_old, m)
        shrink = jnp.exp2(m_old - m)
    p = jnp.exp2(s - m)
    l = jnp.sum(p, axis=0, keepdims=True)
    d = jnp.sum(p * dp, axis=0, keepdims=True)
    if step > 0:
        l = l + l_scr[t] * shrink
        d = d + d_scr[t] * shrink
    m_scr[step, t] = m
    l_scr[t] = l
    d_scr[t] = d
    p_dst[...] = p
    dp_dst[...] = dp


def key_grads(p, dp, factor, delta, q, do, ds_dst):
    n = ds_dst.shape[0]
    p = (p * factor).reshape(n, COLS)
    ds = (p * (dp.reshape(n, COLS) - delta)).astype(jnp.bfloat16)
    ds_dst[...] = ds
    return dot(ds, q, 1, 0), dot(p.astype(jnp.bfloat16), do, 1, 0)


def copy_to(src, dst, send, recv, ctx, head):
    return pltpu.make_async_remote_copy(
        src_ref=src,
        dst_ref=dst,
        send_sem=send,
        recv_sem=recv,
        device_id=(ctx, head),
        device_id_type=MESH,
    )


def backward_kernel(
    n_ctx,
    n_head,
    seq_ref,
    lower_ref,
    q_hbm,
    k_hbm,
    v_hbm,
    do_hbm,
    dq_out,
    dk_ref,
    dv_ref,
    qs,
    dos,
    kv,
    role_k,
    role_v,
    acc,
    p_own,
    dp_own,
    p_far,
    dp_far,
    ds_0,
    ds_1,
    ds_2,
    m_scr,
    l_scr,
    d_scr,
    g1_out,
    g1_in,
    prev_out,
    own_out,
    got_z,
    got_part,
    rest_out,
    got_rest,
    got_x,
    swap_out,
    swap_in,
    load_sem,
    own_sem,
    send_k,
    recv_k,
    send_p,
    recv_p,
    send_f,
    recv_f,
    send_g,
    recv_g,
    send_z,
    recv_z,
    send_x,
    recv_x,
    send_s,
    recv_s,
    send_part,
    recv_part,
    send_rest,
    recv_rest,
):
    me = lax.axis_index("ctx")
    head = lax.axis_index("head")
    core = lax.rem(me, 2)
    partner = me + 1 - 2 * core
    after = lax.rem(me + 2, n_ctx)
    before = lax.rem(me + n_ctx - 2, n_ctx)
    others = [lax.rem(head + s, n_head) for s in range(1, n_head)]
    part = ROWS // n_head

    barrier = pltpu.get_barrier_semaphore()
    senders = [(partner, head), (before, head), (after, head)] + [(after, x) for x in others] + [(me, x) for x in others]
    for ctx, x in senders:
        pl.semaphore_signal(barrier, inc=1, device_id=(ctx, x), device_id_type=MESH)
    loads = []
    for src, dst, i in ((k_hbm, kv.at[0, 0], 0), (v_hbm, kv.at[0, 1], 1)):
        cp = pltpu.make_async_copy(src, dst, own_sem.at[i])
        cp.start()
        loads.append(cp)
    for h in range(HEADS):
        for i, (src, dst) in enumerate(((q_hbm, qs), (do_hbm, dos))):
            cp = pltpu.make_async_copy(
                src.at[:, :, pl.ds(h * WIDTH, WIDTH)], dst.at[:, pl.ds(h * QT, QT), :], load_sem.at[i, h]
            )
            cp.start()
            loads.append(cp)
    pl.semaphore_wait(barrier, len(senders))

    far = []
    for r in range(CHUNKS):
        for which, src in ((0, k_hbm), (1, v_hbm)):
            rows = pl.ds(r * QT, QT)
            i = 2 * r + which
            cp = copy_to(src.at[rows], kv.at[2 + core, which, rows], send_k.at[i], recv_k.at[i], after, head)
            cp.start()
            far.append(cp)
    near = []
    for which, src in ((0, k_hbm), (1, v_hbm)):
        cp = copy_to(src, kv.at[1, which], send_p.at[which], recv_p.at[which], partner, head)
        cp.start()
        near.append(cp)

    own = seq_ref[me]
    odd = lax.rem(own, 2) == 1
    core_is_first = seq_ref[before - core] == own - lax.rem(own, 2) - 2
    base = (own - 2) * ROWS
    stats = (m_scr, l_scr, d_scr)
    for cp in loads:
        cp.wait()
    for t in range(TILES):
        n = (t + 1) * QT
        key_pos = 2 * ROWS + lax.broadcasted_iota(jnp.int32, (n, QT), 0)
        update(
            0, t, kv[0, 0, :n], kv[0, 1, :n], qs[t], dos[t], key_pos, True, lower_ref, base,
            p_own.at[t, pl.ds(0, n)], dp_own.at[t, pl.ds(0, n)], *stats,
        )

    forwards = []

    def pass_on(r):
        rows = pl.ds(r * QT, QT)
        for which in range(2):
            i = 2 * r + which
            far[i].wait_recv()
            place = kv.at[2 + core, which, rows]
            cp = copy_to(place, place, send_f.at[i], recv_f.at[i], partner, head)
            cp.start()
            forwards.append(cp)

    pass_on(0)
    for cp in near:
        cp.wait_recv()
    for r in range(CHUNKS):
        if r + 1 < CHUNKS:
            pass_on(r + 1)
        rows = slice(r * QT, (r + 1) * QT)
        for which, dst in ((0, role_k), (1, role_v)):
            forwards[2 * r + which].wait_recv()
            even_rows = jnp.where(core_is_first, kv[2, which, rows], kv[3, which, rows])
            odd_rows = jnp.where(core_is_first, kv[3, which, rows], kv[2, which, rows])
            dst[r, :QT] = jnp.where(odd, kv[1, which, rows], odd_rows)
            dst[r, QT:] = jnp.where(odd, odd_rows, even_rows)
        for t in range(TILES):
            n = 2 * QT if t <= r else QT
            row = lax.broadcasted_iota(jnp.int32, (n, QT), 0)
            key_pos = r * QT + row + jnp.where(row < QT, ROWS, -QT)
            update(
                r + 1, t, role_k[r, :n], role_v[r, :n], qs[t], dos[t], key_pos, False, lower_ref, base,
                p_far.at[r, t, pl.ds(0, n)], dp_far.at[r, t, pl.ds(0, n)], *stats,
            )

    for t in range(TILES):
        inv = 1.0 / l_scr[t]
        l_scr[t] = inv
        d_scr[t] = d_scr[t] * inv
    for t in range(TILES):
        factor = jnp.exp2(m_scr[1:, t] - m_scr[CHUNKS, t][None]) * l_scr[t][None]
        dk, dv = key_grads(p_far[:, t, :QT], dp_far[:, t, :QT], factor, d_scr[t], qs[t], dos[t], ds_1.at[t])
        if t == 0:
            acc[1, :, :WIDTH] = dk
            acc[1, :, WIDTH:] = dv
        else:
            acc[1, :, :WIDTH] += dk
            acc[1, :, WIDTH:] += dv

    def grads(role):
        return jnp.concatenate([acc[role, :, :WIDTH] * SCALE, acc[role, :, WIDTH:]], axis=1)

    g1_out[...] = grads(1).astype(jnp.bfloat16)
    trade = copy_to(g1_out, g1_in, send_g, recv_g, partner, head)
    trade.start()
    for t in range(TILES):
        f = t * QT
        factor = jnp.exp2(m_scr[1 + t :, t] - m_scr[CHUNKS, t][None]) * l_scr[t][None]
        dk, dv = key_grads(
            p_far[t:, t, QT:], dp_far[t:, t, QT:], factor, d_scr[t], qs[t], dos[t], ds_2.at[t, pl.ds(f, ROWS - f)]
        )
        if t == 0:
            acc[2, :, :WIDTH] = dk
            acc[2, :, WIDTH:] = dv
        else:
            acc[2, f:, :WIDTH] += dk
            acc[2, f:, WIDTH:] += dv
    trade.wait_recv()
    none = jnp.zeros((ROWS, 2 * WIDTH), jnp.float32)
    traded = g1_in[...].astype(jnp.float32)
    prev_out[...] = (grads(2) + jnp.where(odd, traded, none)).astype(jnp.bfloat16)
    summed = []
    for s in range(1, n_head):
        x = lax.rem(head + s, n_head)
        some = pl.ds(pl.multiple_of(x * part + STRAIGHT, 16), part - STRAIGHT)
        cp = copy_to(prev_out.at[some], got_part.at[s - 1], send_part.at[s - 1], recv_part.at[s - 1], me, x)
        cp.start()
        summed.append(cp)
    back = []
    for s in range(n_head):
        x = lax.rem(head + s, n_head)
        some = pl.ds(pl.multiple_of(x * part, part), STRAIGHT)
        cp = copy_to(prev_out.at[some], got_z.at[s], send_z.at[s], recv_z.at[s], before, x)
        cp.start()
        back.append(cp)
    for t in reversed(range(TILES)):
        n = (t + 1) * QT
        factor = jnp.exp2(m_scr[0, t] - m_scr[CHUNKS, t]) * l_scr[t]
        dk, dv = key_grads(
            p_own[t, :n], dp_own[t, :n], factor, d_scr[t], qs[t], dos[t], ds_0.at[t, pl.ds(0, n)]
        )
        if t == TILES - 1:
            acc[0, :, :WIDTH] = dk
            acc[0, :, WIDTH:] = dv
        else:
            acc[0, :n, :WIDTH] += dk
            acc[0, :n, WIDTH:] += dv
    acc[0] = grads(0) + jnp.where(odd, none, g1_in[...].astype(jnp.float32))
    own_out[...] = acc[0].astype(jnp.bfloat16)
    across = []
    for s in range(1, n_head):
        x = lax.rem(head + s, n_head)
        cp = copy_to(own_out.at[pl.ds(x * part, part)], got_x.at[s - 1], send_x.at[s - 1], recv_x.at[s - 1], me, x)
        cp.start()
        across.append(cp)
    for t in range(TILES):
        n = (t + 1) * QT
        f = t * QT
        k1 = role_k[:, :QT].reshape(ROWS, WIDTH)
        k2 = role_k[t:, QT:].reshape(ROWS - f, WIDTH)
        dq = dot(kv[0, 0, :n], ds_0[t, :n], 0, 0) + dot(k1, ds_1[t], 0, 0) + dot(k2, ds_2[t, f:], 0, 0)
        dq = dq * SCALE
        rows = pl.ds(t * QT, QT)
        for h in range(HEADS):
            dq_out[rows, h * WIDTH : (h + 1) * WIDTH] = dq[:, h * QT : (h + 1) * QT].T.astype(dq_out.dtype)
    for cp in summed:
        cp.wait_recv()
    some = pl.ds(pl.multiple_of(head * part + STRAIGHT, 16), part - STRAIGHT)
    rest = prev_out[some, :].astype(jnp.float32)
    for s in range(n_head - 1):
        rest = rest + got_part[s].astype(jnp.float32)
    rest_out[...] = rest.astype(jnp.bfloat16)
    cp = copy_to(rest_out, got_rest, send_rest, recv_rest, before, head)
    cp.start()
    back.append(cp)
    for cp in back:
        cp.wait_recv()
    came = got_z[0].astype(jnp.float32)
    for s in range(1, n_head):
        came = came + got_z[s].astype(jnp.float32)
    came = jnp.concatenate([came, got_rest[...].astype(jnp.float32)], axis=0)
    swap_out[...] = came.astype(jnp.bfloat16)
    swap = copy_to(swap_out, swap_in, send_s, recv_s, partner, head)
    swap.start()
    total = acc[0, pl.ds(head * part, part), :]
    for cp in across:
        cp.wait_recv()
    for s in range(n_head - 1):
        total = total + got_x[s].astype(jnp.float32)
    swap.wait_recv()
    straight = lax.rem(seq_ref[after], 2) == lax.rem(own, 2)
    total = total + jnp.where(straight, came, swap_in[...].astype(jnp.float32))
    dk_ref[...] = total[:, :WIDTH].astype(jnp.bfloat16)
    dv_ref[...] = total[:, WIDTH:].astype(jnp.bfloat16)
    for cp in far + near + forwards + [trade] + summed + back + across + [swap]:
        cp.wait_send()


def hand_on_kernel(dq_ref, dk_ref, dv_ref, dq_out, dk_out, dv_out, sem):
    copies = []
    for i, (src, dst) in enumerate(((dq_ref, dq_out), (dk_ref, dk_out), (dv_ref, dv_out))):
        cp = pltpu.make_async_copy(src, dst, sem.at[i])
        cp.start()
        copies.append(cp)
    for cp in copies:
        cp.wait()


def shards(queries, keys, values, out_grad, doc_start, block_seq):
    n_ctx = lax.axis_size("ctx")
    n_head = lax.axis_size("head")
    part = ROWS // n_head
    smem = pl.BlockSpec(memory_space=pltpu.SMEM)
    vmem = pl.BlockSpec(memory_space=pltpu.VMEM)
    hbm = pl.BlockSpec(memory_space=pltpu.HBM)
    f32 = jnp.float32
    bf16 = jnp.bfloat16
    dma = pltpu.SemaphoreType.DMA
    grads = pl.pallas_call(
        functools.partial(backward_kernel, n_ctx, n_head),
        out_shape=(
            pltpu.VMEM(queries.shape, bf16),
            pltpu.VMEM((part, WIDTH), bf16),
            pltpu.VMEM((part, WIDTH), bf16),
        ),
        in_specs=[smem, vmem, hbm, hbm, hbm, hbm],
        out_specs=(vmem, vmem, vmem),
        scratch_shapes=[
            pltpu.VMEM((TILES, COLS, WIDTH), bf16),
            pltpu.VMEM((TILES, COLS, WIDTH), bf16),
            pltpu.VMEM((4, 2, ROWS, WIDTH), bf16),
            pltpu.VMEM((CHUNKS, 2 * QT, WIDTH), bf16),
            pltpu.VMEM((CHUNKS, 2 * QT, WIDTH), bf16),
            pltpu.VMEM((3, ROWS, 2 * WIDTH), f32),
            pltpu.VMEM((TILES, ROWS, COLS), f32),
            pltpu.VMEM((TILES, ROWS, COLS), f32),
            pltpu.VMEM((CHUNKS, TILES, 2 * QT, COLS), f32),
            pltpu.VMEM((CHUNKS, TILES, 2 * QT, COLS), f32),
            pltpu.VMEM((TILES, ROWS, COLS), bf16),
            pltpu.VMEM((TILES, ROWS, COLS), bf16),
            pltpu.VMEM((TILES, ROWS, COLS), bf16),
            pltpu.VMEM((CHUNKS + 1, TILES, 1, COLS), f32),
            pltpu.VMEM((TILES, 1, COLS), f32),
            pltpu.VMEM((TILES, 1, COLS), f32),
            pltpu.VMEM((ROWS, 2 * WIDTH), bf16),
            pltpu.VMEM((ROWS, 2 * WIDTH), bf16),
            pltpu.VMEM((ROWS, 2 * WIDTH), bf16),
            pltpu.VMEM((ROWS, 2 * WIDTH), bf16),
            pltpu.VMEM((n_head, STRAIGHT, 2 * WIDTH), bf16),
            pltpu.VMEM((n_head - 1, part - STRAIGHT, 2 * WIDTH), bf16),
            pltpu.VMEM((part - STRAIGHT, 2 * WIDTH), bf16),
            pltpu.VMEM((part - STRAIGHT, 2 * WIDTH), bf16),
            pltpu.VMEM((n_head - 1, part, 2 * WIDTH), bf16),
            pltpu.VMEM((part, 2 * WIDTH), bf16),
            pltpu.VMEM((part, 2 * WIDTH), bf16),
            dma((2, HEADS)),
            dma((2,)),
            dma((2 * CHUNKS,)),
            dma((2 * CHUNKS,)),
            dma((2,)),
            dma((2,)),
            dma((2 * CHUNKS,)),
            dma((2 * CHUNKS,)),
            dma,
            dma,
            dma((n_head,)),
            dma((n_head,)),
            dma((n_head - 1,)),
            dma((n_head - 1,)),
            dma,
            dma,
            dma((n_head - 1,)),
            dma((n_head - 1,)),
            dma,
            dma,
        ],
        compiler_params=pltpu.CompilerParams(
            collective_id=0, has_side_effects=True, vmem_limit_bytes=VMEM_LIMIT
        ),
        name="backward",
    )(
        block_seq,
        doc_start.reshape(TILES, QT),
        queries.reshape(TILES, QT, HEADS * WIDTH),
        keys,
        values,
        out_grad.reshape(TILES, QT, HEADS * WIDTH),
    )
    return pl.pallas_call(
        hand_on_kernel,
        out_shape=tuple(jax.ShapeDtypeStruct(g.shape, g.dtype) for g in grads),
        in_specs=[vmem] * 3,
        out_specs=(hbm,) * 3,
        scratch_shapes=[dma((3,))],
        compiler_params=pltpu.CompilerParams(vmem_limit_bytes=1024 * 1024),
        name="hand_on",
    )(*grads)


def solution(mesh):
    return jax.shard_map(
        shards,
        mesh=mesh,
        in_specs=(
            P("ctx", "head"),
            P("ctx", None),
            P("ctx", None),
            P("ctx", "head"),
            P("ctx"),
            P(),
        ),
        out_specs=(P("ctx", "head"), P(("ctx", "head"), None), P(("ctx", "head"), None)),
        check_vma=False,
    )
```

```python
import functools
import math

import jax
import jax.numpy as jnp
from jax import lax
from jax.experimental import pallas as pl
from jax.experimental.pallas import tpu as pltpu
from jax.sharding import PartitionSpec as P

MESH = pl.DeviceIdType.MESH

ROWS = 512
WIDTH = 128
HEADS = 4
QT = 128
TILES = ROWS // QT
COLS = HEADS * QT
MASKED = -1e30
CHUNKS = TILES
STRAIGHT = 80
VMEM_LIMIT = 59 * 1024 * 1024 + 512 * 1024
SCALE = WIDTH ** (-0.5)
SCALE2 = SCALE * math.log2(math.e)


def dot(a, b, ca, cb):
    return lax.dot_general(a, b, (((ca,), (cb,)), ((), ())), preferred_element_type=jnp.float32)


def update(step, t, k, v, q, do, key_pos, causal, lower_ref, base, p_dst, dp_dst, m_scr, l_scr, d_scr):
    row_pos = 2 * ROWS + t * QT + lax.broadcasted_iota(jnp.int32, (1, QT), 1)
    lower = jnp.clip(lower_ref[pl.ds(t, 1), :] - base, jnp.maximum(row_pos - 2 * ROWS + 1, -base), row_pos)
    seen = key_pos >= lower
    if causal:
        seen = seen & (key_pos <= row_pos)
    bias = jnp.where(seen, 0.0, MASKED)
    s = dot(k, q, 1, 1) * SCALE2 + jnp.concatenate([bias] * HEADS, axis=1)
    dp = dot(v, do, 1, 1)
    m = jnp.max(s, axis=0, keepdims=True)
    if step > 0:
        m_old = m_scr[step - 1, t]
        m = jnp.maximum(m_old, m)
        shrink = jnp.exp2(m_old - m)
    p = jnp.exp2(s - m)
    l = jnp.sum(p, axis=0, keepdims=True)
    d = jnp.sum(p * dp, axis=0, keepdims=True)
    if step > 0:
        l = l + l_scr[t] * shrink
        d = d + d_scr[t] * shrink
    m_scr[step, t] = m
    l_scr[t] = l
    d_scr[t] = d
    p_dst[...] = p
    dp_dst[...] = dp


def key_grads(p, dp, factor, delta, q, do, ds_dst):
    n = ds_dst.shape[0]
    p = (p * factor).reshape(n, COLS)
    ds = (p * (dp.reshape(n, COLS) - delta)).astype(jnp.bfloat16)
    ds_dst[...] = ds
    return dot(ds, q, 1, 0), dot(p.astype(jnp.bfloat16), do, 1, 0)


def copy_to(src, dst, send, recv, ctx, head):
    return pltpu.make_async_remote_copy(
        src_ref=src,
        dst_ref=dst,
        send_sem=send,
        recv_sem=recv,
        device_id=(ctx, head),
        device_id_type=MESH,
    )


def backward_kernel(
    n_ctx,
    n_head,
    seq_ref,
    lower_ref,
    q_hbm,
    k_hbm,
    v_hbm,
    do_hbm,
    dq_out,
    dk_ref,
    dv_ref,
    qs,
    dos,
    kv,
    role_k,
    role_v,
    acc,
    p_own,
    dp_own,
    p_far,
    dp_far,
    ds_0,
    ds_1,
    ds_2,
    m_scr,
    l_scr,
    d_scr,
    g1_out,
    g1_in,
    prev_out,
    own_out,
    got_z,
    got_part,
    rest_out,
    got_rest,
    got_x,
    swap_out,
    swap_in,
    load_sem,
    own_sem,
    send_k,
    recv_k,
    send_p,
    recv_p,
    send_f,
    recv_f,
    send_g,
    recv_g,
    send_z,
    recv_z,
    send_x,
    recv_x,
    send_s,
    recv_s,
    send_part,
    recv_part,
    send_rest,
    recv_rest,
):
    me = lax.axis_index("ctx")
    head = lax.axis_index("head")
    core = lax.rem(me, 2)
    partner = me + 1 - 2 * core
    after = lax.rem(me + 2, n_ctx)
    before = lax.rem(me + n_ctx - 2, n_ctx)
    others = [lax.rem(head + s, n_head) for s in range(1, n_head)]
    part = ROWS // n_head

    barrier = pltpu.get_barrier_semaphore()
    senders = [(partner, head), (before, head), (after, head)] + [(after, x) for x in others] + [(me, x) for x in others]
    for ctx, x in senders:
        pl.semaphore_signal(barrier, inc=1, device_id=(ctx, x), device_id_type=MESH)
    loads = []
    for src, dst, i in ((k_hbm, kv.at[0, 0], 0), (v_hbm, kv.at[0, 1], 1)):
        cp = pltpu.make_async_copy(src, dst, own_sem.at[i])
        cp.start()
        loads.append(cp)
    for h in range(HEADS):
        for i, (src, dst) in enumerate(((q_hbm, qs), (do_hbm, dos))):
            cp = pltpu.make_async_copy(
                src.at[:, :, pl.ds(h * WIDTH, WIDTH)], dst.at[:, pl.ds(h * QT, QT), :], load_sem.at[i, h]
            )
            cp.start()
            loads.append(cp)
    pl.semaphore_wait(barrier, len(senders))

    far = []
    for r in range(CHUNKS):
        for which, src in ((0, k_hbm), (1, v_hbm)):
            rows = pl.ds(r * QT, QT)
            i = 2 * r + which
            cp = copy_to(src.at[rows], kv.at[2 + core, which, rows], send_k.at[i], recv_k.at[i], after, head)
            cp.start()
            far.append(cp)
    near = []
    for which, src in ((0, k_hbm), (1, v_hbm)):
        cp = copy_to(src, kv.at[1, which], send_p.at[which], recv_p.at[which], partner, head)
        cp.start()
        near.append(cp)

    own = seq_ref[me]
    odd = lax.rem(own, 2) == 1
    core_is_first = seq_ref[before - core] == own - lax.rem(own, 2) - 2
    base = (own - 2) * ROWS
    stats = (m_scr, l_scr, d_scr)
    for cp in loads:
        cp.wait()
    for t in range(TILES):
        n = (t + 1) * QT
        key_pos = 2 * ROWS + lax.broadcasted_iota(jnp.int32, (n, QT), 0)
        update(
            0, t, kv[0, 0, :n], kv[0, 1, :n], qs[t], dos[t], key_pos, True, lower_ref, base,
            p_own.at[t, pl.ds(0, n)], dp_own.at[t, pl.ds(0, n)], *stats,
        )

    forwards = []

    def pass_on(r):
        rows = pl.ds(r * QT, QT)
        for which in range(2):
            i = 2 * r + which
            far[i].wait_recv()
            place = kv.at[2 + core, which, rows]
            cp = copy_to(place, place, send_f.at[i], recv_f.at[i], partner, head)
            cp.start()
            forwards.append(cp)

    pass_on(0)
    for cp in near:
        cp.wait_recv()
    for r in range(CHUNKS):
        if r + 1 < CHUNKS:
            pass_on(r + 1)
        rows = slice(r * QT, (r + 1) * QT)
        for which, dst in ((0, role_k), (1, role_v)):
            forwards[2 * r + which].wait_recv()
            even_rows = jnp.where(core_is_first, kv[2, which, rows], kv[3, which, rows])
            odd_rows = jnp.where(core_is_first, kv[3, which, rows], kv[2, which, rows])
            dst[r, :QT] = jnp.where(odd, kv[1, which, rows], odd_rows)
            dst[r, QT:] = jnp.where(odd, odd_rows, even_rows)
        for t in range(TILES):
            n = 2 * QT if t <= r else QT
            row = lax.broadcasted_iota(jnp.int32, (n, QT), 0)
            key_pos = r * QT + row + jnp.where(row < QT, ROWS, -QT)
            update(
                r + 1, t, role_k[r, :n], role_v[r, :n], qs[t], dos[t], key_pos, False, lower_ref, base,
                p_far.at[r, t, pl.ds(0, n)], dp_far.at[r, t, pl.ds(0, n)], *stats,
            )

    for t in range(TILES):
        inv = 1.0 / l_scr[t]
        l_scr[t] = inv
        d_scr[t] = d_scr[t] * inv
    for t in range(TILES):
        factor = jnp.exp2(m_scr[1:, t] - m_scr[CHUNKS, t][None]) * l_scr[t][None]
        dk, dv = key_grads(p_far[:, t, :QT], dp_far[:, t, :QT], factor, d_scr[t], qs[t], dos[t], ds_1.at[t])
        if t == 0:
            acc[1, :, :WIDTH] = dk
            acc[1, :, WIDTH:] = dv
        else:
            acc[1, :, :WIDTH] += dk
            acc[1, :, WIDTH:] += dv

    def grads(role):
        return jnp.concatenate([acc[role, :, :WIDTH] * SCALE, acc[role, :, WIDTH:]], axis=1)

    g1_out[...] = grads(1).astype(jnp.bfloat16)
    trade = copy_to(g1_out, g1_in, send_g, recv_g, partner, head)
    trade.start()
    for t in range(TILES):
        f = t * QT
        factor = jnp.exp2(m_scr[1 + t :, t] - m_scr[CHUNKS, t][None]) * l_scr[t][None]
        dk, dv = key_grads(
            p_far[t:, t, QT:], dp_far[t:, t, QT:], factor, d_scr[t], qs[t], dos[t], ds_2.at[t, pl.ds(f, ROWS - f)]
        )
        if t == 0:
            acc[2, :, :WIDTH] = dk
            acc[2, :, WIDTH:] = dv
        else:
            acc[2, f:, :WIDTH] += dk
            acc[2, f:, WIDTH:] += dv
    trade.wait_recv()
    none = jnp.zeros((ROWS, 2 * WIDTH), jnp.float32)
    traded = g1_in[...].astype(jnp.float32)
    prev_out[...] = (grads(2) + jnp.where(odd, traded, none)).astype(jnp.bfloat16)
    summed = []
    for s in range(1, n_head):
        x = lax.rem(head + s, n_head)
        some = pl.ds(pl.multiple_of(x * part + STRAIGHT, 16), part - STRAIGHT)
        cp = copy_to(prev_out.at[some], got_part.at[s - 1], send_part.at[s - 1], recv_part.at[s - 1], me, x)
        cp.start()
        summed.append(cp)
    back = []
    for s in range(n_head):
        x = lax.rem(head + s, n_head)
        some = pl.ds(pl.multiple_of(x * part, part), STRAIGHT)
        cp = copy_to(prev_out.at[some], got_z.at[s], send_z.at[s], recv_z.at[s], before, x)
        cp.start()
        back.append(cp)
    for t in reversed(range(TILES)):
        n = (t + 1) * QT
        factor = jnp.exp2(m_scr[0, t] - m_scr[CHUNKS, t]) * l_scr[t]
        dk, dv = key_grads(
            p_own[t, :n], dp_own[t, :n], factor, d_scr[t], qs[t], dos[t], ds_0.at[t, pl.ds(0, n)]
        )
        if t == TILES - 1:
            acc[0, :, :WIDTH] = dk
            acc[0, :, WIDTH:] = dv
        else:
            acc[0, :n, :WIDTH] += dk
            acc[0, :n, WIDTH:] += dv
    acc[0] = grads(0) + jnp.where(odd, none, g1_in[...].astype(jnp.float32))
    own_out[...] = acc[0].astype(jnp.bfloat16)
    across = []
    for s in range(1, n_head):
        x = lax.rem(head + s, n_head)
        cp = copy_to(own_out.at[pl.ds(x * part, part)], got_x.at[s - 1], send_x.at[s - 1], recv_x.at[s - 1], me, x)
        cp.start()
        across.append(cp)
    for cp in summed:
        cp.wait_recv()
    some = pl.ds(pl.multiple_of(head * part + STRAIGHT, 16), part - STRAIGHT)
    rest = prev_out[some, :].astype(jnp.float32)
    for s in range(n_head - 1):
        rest = rest + got_part[s].astype(jnp.float32)
    rest_out[...] = rest.astype(jnp.bfloat16)
    cp = copy_to(rest_out, got_rest, send_rest, recv_rest, before, head)
    cp.start()
    back.append(cp)
    for t in range(TILES):
        n = (t + 1) * QT
        f = t * QT
        k1 = role_k[:, :QT].reshape(ROWS, WIDTH)
        k2 = role_k[t:, QT:].reshape(ROWS - f, WIDTH)
        dq = dot(kv[0, 0, :n], ds_0[t, :n], 0, 0) + dot(k1, ds_1[t], 0, 0) + dot(k2, ds_2[t, f:], 0, 0)
        dq = dq * SCALE
        rows = pl.ds(t * QT, QT)
        for h in range(HEADS):
            dq_out[rows, h * WIDTH : (h + 1) * WIDTH] = dq[:, h * QT : (h + 1) * QT].T.astype(dq_out.dtype)
    for cp in back:
        cp.wait_recv()
    came = got_z[0].astype(jnp.float32)
    for s in range(1, n_head):
        came = came + got_z[s].astype(jnp.float32)
    came = jnp.concatenate([came, got_rest[...].astype(jnp.float32)], axis=0)
    swap_out[...] = came.astype(jnp.bfloat16)
    swap = copy_to(swap_out, swap_in, send_s, recv_s, partner, head)
    swap.start()
    total = acc[0, pl.ds(head * part, part), :]
    for cp in across:
        cp.wait_recv()
    for s in range(n_head - 1):
        total = total + got_x[s].astype(jnp.float32)
    swap.wait_recv()
    straight = lax.rem(seq_ref[after], 2) == lax.rem(own, 2)
    total = total + jnp.where(straight, came, swap_in[...].astype(jnp.float32))
    dk_ref[...] = total[:, :WIDTH].astype(jnp.bfloat16)
    dv_ref[...] = total[:, WIDTH:].astype(jnp.bfloat16)
    for cp in far + near + forwards + [trade] + summed + back + across + [swap]:
        cp.wait_send()


def hand_on_kernel(dq_ref, dk_ref, dv_ref, dq_out, dk_out, dv_out, sem):
    copies = []
    for i, (src, dst) in enumerate(((dq_ref, dq_out), (dk_ref, dk_out), (dv_ref, dv_out))):
        cp = pltpu.make_async_copy(src, dst, sem.at[i])
        cp.start()
        copies.append(cp)
    for cp in copies:
        cp.wait()


def shards(queries, keys, values, out_grad, doc_start, block_seq):
    n_ctx = lax.axis_size("ctx")
    n_head = lax.axis_size("head")
    part = ROWS // n_head
    smem = pl.BlockSpec(memory_space=pltpu.SMEM)
    vmem = pl.BlockSpec(memory_space=pltpu.VMEM)
    hbm = pl.BlockSpec(memory_space=pltpu.HBM)
    f32 = jnp.float32
    bf16 = jnp.bfloat16
    dma = pltpu.SemaphoreType.DMA
    grads = pl.pallas_call(
        functools.partial(backward_kernel, n_ctx, n_head),
        out_shape=(
            pltpu.VMEM(queries.shape, bf16),
            pltpu.VMEM((part, WIDTH), bf16),
            pltpu.VMEM((part, WIDTH), bf16),
        ),
        in_specs=[smem, vmem, hbm, hbm, hbm, hbm],
        out_specs=(vmem, vmem, vmem),
        scratch_shapes=[
            pltpu.VMEM((TILES, COLS, WIDTH), bf16),
            pltpu.VMEM((TILES, COLS, WIDTH), bf16),
            pltpu.VMEM((4, 2, ROWS, WIDTH), bf16),
            pltpu.VMEM((CHUNKS, 2 * QT, WIDTH), bf16),
            pltpu.VMEM((CHUNKS, 2 * QT, WIDTH), bf16),
            pltpu.VMEM((3, ROWS, 2 * WIDTH), f32),
            pltpu.VMEM((TILES, ROWS, COLS), f32),
            pltpu.VMEM((TILES, ROWS, COLS), f32),
            pltpu.VMEM((CHUNKS, TILES, 2 * QT, COLS), f32),
            pltpu.VMEM((CHUNKS, TILES, 2 * QT, COLS), f32),
            pltpu.VMEM((TILES, ROWS, COLS), bf16),
            pltpu.VMEM((TILES, ROWS, COLS), bf16),
            pltpu.VMEM((TILES, ROWS, COLS), bf16),
            pltpu.VMEM((CHUNKS + 1, TILES, 1, COLS), f32),
            pltpu.VMEM((TILES, 1, COLS), f32),
            pltpu.VMEM((TILES, 1, COLS), f32),
            pltpu.VMEM((ROWS, 2 * WIDTH), bf16),
            pltpu.VMEM((ROWS, 2 * WIDTH), bf16),
            pltpu.VMEM((ROWS, 2 * WIDTH), bf16),
            pltpu.VMEM((ROWS, 2 * WIDTH), bf16),
            pltpu.VMEM((n_head, STRAIGHT, 2 * WIDTH), bf16),
            pltpu.VMEM((n_head - 1, part - STRAIGHT, 2 * WIDTH), bf16),
            pltpu.VMEM((part - STRAIGHT, 2 * WIDTH), bf16),
            pltpu.VMEM((part - STRAIGHT, 2 * WIDTH), bf16),
            pltpu.VMEM((n_head - 1, part, 2 * WIDTH), bf16),
            pltpu.VMEM((part, 2 * WIDTH), bf16),
            pltpu.VMEM((part, 2 * WIDTH), bf16),
            dma((2, HEADS)),
            dma((2,)),
            dma((2 * CHUNKS,)),
            dma((2 * CHUNKS,)),
            dma((2,)),
            dma((2,)),
            dma((2 * CHUNKS,)),
            dma((2 * CHUNKS,)),
            dma,
            dma,
            dma((n_head,)),
            dma((n_head,)),
            dma((n_head - 1,)),
            dma((n_head - 1,)),
            dma,
            dma,
            dma((n_head - 1,)),
            dma((n_head - 1,)),
            dma,
            dma,
        ],
        compiler_params=pltpu.CompilerParams(
            collective_id=0, has_side_effects=True, vmem_limit_bytes=VMEM_LIMIT
        ),
        name="backward",
    )(
        block_seq,
        doc_start.reshape(TILES, QT),
        queries.reshape(TILES, QT, HEADS * WIDTH),
        keys,
        values,
        out_grad.reshape(TILES, QT, HEADS * WIDTH),
    )
    return pl.pallas_call(
        hand_on_kernel,
        out_shape=tuple(jax.ShapeDtypeStruct(g.shape, g.dtype) for g in grads),
        in_specs=[vmem] * 3,
        out_specs=(hbm,) * 3,
        scratch_shapes=[dma((3,))],
        compiler_params=pltpu.CompilerParams(vmem_limit_bytes=1024 * 1024),
        name="hand_on",
    )(*grads)


def solution(mesh):
    return jax.shard_map(
        shards,
        mesh=mesh,
        in_specs=(
            P("ctx", "head"),
            P("ctx", None),
            P("ctx", None),
            P("ctx", "head"),
            P("ctx"),
            P(),
        ),
        out_specs=(P("ctx", "head"), P(("ctx", "head"), None), P(("ctx", "head"), None)),
        check_vma=False,
    )
```

```python
import functools
import math

import jax
import jax.numpy as jnp
from jax import lax
from jax.experimental import pallas as pl
from jax.experimental.pallas import tpu as pltpu
from jax.sharding import PartitionSpec as P

MESH = pl.DeviceIdType.MESH

ROWS = 512
WIDTH = 128
HEADS = 4
QT = 128
TILES = ROWS // QT
COLS = HEADS * QT
MASKED = -1e30
CHUNKS = TILES
STRAIGHT = 80
VMEM_LIMIT = 59 * 1024 * 1024 + 512 * 1024
SCALE = WIDTH ** (-0.5)
SCALE2 = SCALE * math.log2(math.e)


def dot(a, b, ca, cb):
    return lax.dot_general(a, b, (((ca,), (cb,)), ((), ())), preferred_element_type=jnp.float32)


def update(step, t, k, v, q, do, key_pos, causal, lower_ref, base, p_dst, dp_dst, m_scr, l_scr, d_scr):
    row_pos = 2 * ROWS + t * QT + lax.broadcasted_iota(jnp.int32, (1, QT), 1)
    lower = jnp.clip(lower_ref[pl.ds(t, 1), :] - base, jnp.maximum(row_pos - 2 * ROWS + 1, -base), row_pos)
    seen = key_pos >= lower
    if causal:
        seen = seen & (key_pos <= row_pos)
    bias = jnp.where(seen, 0.0, MASKED)
    s = dot(k, q, 1, 1) * SCALE2 + jnp.concatenate([bias] * HEADS, axis=1)
    dp = dot(v, do, 1, 1)
    m = jnp.max(s, axis=0, keepdims=True)
    if step > 0:
        m_old = m_scr[0 if step == CHUNKS else step + 1, t]
        m = jnp.maximum(m_old, m)
        shrink = jnp.exp2(m_old - m)
    p = jnp.exp2(s - m)
    l = jnp.sum(p, axis=0, keepdims=True)
    d = jnp.sum(p * dp, axis=0, keepdims=True)
    if step > 0:
        l = l + l_scr[t] * shrink
        d = d + d_scr[t] * shrink
    m_scr[step, t] = m
    l_scr[t] = l
    d_scr[t] = d
    p_dst[...] = p
    dp_dst[...] = dp


def key_grads(p, dp, factor, delta, q, do, ds_dst):
    n = ds_dst.shape[0]
    p = (p * factor).reshape(n, COLS)
    ds = (p * (dp.reshape(n, COLS) - delta)).astype(jnp.bfloat16)
    ds_dst[...] = ds
    return dot(ds, q, 1, 0), dot(p.astype(jnp.bfloat16), do, 1, 0)


def copy_to(src, dst, send, recv, ctx, head):
    return pltpu.make_async_remote_copy(
        src_ref=src,
        dst_ref=dst,
        send_sem=send,
        recv_sem=recv,
        device_id=(ctx, head),
        device_id_type=MESH,
    )


def backward_kernel(
    n_ctx,
    n_head,
    seq_ref,
    lower_ref,
    q_hbm,
    k_hbm,
    v_hbm,
    do_hbm,
    dq_out,
    dk_ref,
    dv_ref,
    qs,
    dos,
    kv,
    role_k,
    role_v,
    acc,
    p_own,
    dp_own,
    p_far,
    dp_far,
    ds_0,
    ds_1,
    ds_2,
    m_scr,
    l_scr,
    d_scr,
    g1_out,
    g1_in,
    prev_out,
    own_out,
    got_z,
    got_part,
    rest_out,
    got_rest,
    got_x,
    swap_out,
    swap_in,
    load_sem,
    own_sem,
    send_k,
    recv_k,
    send_p,
    recv_p,
    send_f,
    recv_f,
    send_g,
    recv_g,
    send_z,
    recv_z,
    send_x,
    recv_x,
    send_s,
    recv_s,
    send_part,
    recv_part,
    send_rest,
    recv_rest,
):
    me = lax.axis_index("ctx")
    head = lax.axis_index("head")
    core = lax.rem(me, 2)
    partner = me + 1 - 2 * core
    after = lax.rem(me + 2, n_ctx)
    before = lax.rem(me + n_ctx - 2, n_ctx)
    others = [lax.rem(head + s, n_head) for s in range(1, n_head)]
    part = ROWS // n_head

    barrier = pltpu.get_barrier_semaphore()
    senders = [(partner, head), (before, head), (after, head)] + [(after, x) for x in others] + [(me, x) for x in others]
    for ctx, x in senders:
        pl.semaphore_signal(barrier, inc=1, device_id=(ctx, x), device_id_type=MESH)
    loads = []
    for src, dst, i in ((k_hbm, kv.at[0, 0], 0), (v_hbm, kv.at[0, 1], 1)):
        cp = pltpu.make_async_copy(src, dst, own_sem.at[i])
        cp.start()
        loads.append(cp)
    for h in range(HEADS):
        for i, (src, dst) in enumerate(((q_hbm, qs), (do_hbm, dos))):
            cp = pltpu.make_async_copy(
                src.at[:, :, pl.ds(h * WIDTH, WIDTH)], dst.at[:, pl.ds(h * QT, QT), :], load_sem.at[i, h]
            )
            cp.start()
            loads.append(cp)
    pl.semaphore_wait(barrier, len(senders))

    far = {}
    for r in reversed(range(CHUNKS)):
        for which, src in ((0, k_hbm), (1, v_hbm)):
            rows = pl.ds(r * QT, QT)
            i = 2 * r + which
            cp = copy_to(src.at[rows], kv.at[2 + core, which, rows], send_k.at[i], recv_k.at[i], after, head)
            cp.start()
            far[i] = cp
    near = []
    for which, src in ((0, k_hbm), (1, v_hbm)):
        cp = copy_to(src, kv.at[1, which], send_p.at[which], recv_p.at[which], partner, head)
        cp.start()
        near.append(cp)

    own = seq_ref[me]
    odd = lax.rem(own, 2) == 1
    core_is_first = seq_ref[before - core] == own - lax.rem(own, 2) - 2
    base = (own - 2) * ROWS
    stats = (m_scr, l_scr, d_scr)
    for cp in loads:
        cp.wait()
    for t in range(TILES):
        n = (t + 1) * QT
        key_pos = 2 * ROWS + lax.broadcasted_iota(jnp.int32, (n, QT), 0)
        update(
            0, t, kv[0, 0, :n], kv[0, 1, :n], qs[t], dos[t], key_pos, True, lower_ref, base,
            p_own.at[t, pl.ds(0, n)], dp_own.at[t, pl.ds(0, n)], *stats,
        )

    forwards = {}

    def pass_on(r):
        rows = pl.ds(r * QT, QT)
        for which in range(2):
            i = 2 * r + which
            far[i].wait_recv()
            place = kv.at[2 + core, which, rows]
            cp = copy_to(place, place, send_f.at[i], recv_f.at[i], partner, head)
            cp.start()
            forwards[i] = cp

    pass_on(CHUNKS - 1)
    for cp in near:
        cp.wait_recv()
    for r in reversed(range(CHUNKS)):
        if r > 0:
            pass_on(r - 1)
        rows = slice(r * QT, (r + 1) * QT)
        for which, dst in ((0, role_k), (1, role_v)):
            forwards[2 * r + which].wait_recv()
            even_rows = jnp.where(core_is_first, kv[2, which, rows], kv[3, which, rows])
            odd_rows = jnp.where(core_is_first, kv[3, which, rows], kv[2, which, rows])
            dst[r, :QT] = jnp.where(odd, kv[1, which, rows], odd_rows)
            dst[r, QT:] = jnp.where(odd, odd_rows, even_rows)
        for t in range(TILES):
            n = 2 * QT if t <= r else QT
            row = lax.broadcasted_iota(jnp.int32, (n, QT), 0)
            key_pos = r * QT + row + jnp.where(row < QT, ROWS, -QT)
            update(
                r + 1, t, role_k[r, :n], role_v[r, :n], qs[t], dos[t], key_pos, False, lower_ref, base,
                p_far.at[r, t, pl.ds(0, n)], dp_far.at[r, t, pl.ds(0, n)], *stats,
            )

    for t in range(TILES):
        inv = 1.0 / l_scr[t]
        l_scr[t] = inv
        d_scr[t] = d_scr[t] * inv
    for t in range(TILES):
        factor = jnp.exp2(m_scr[1:, t] - m_scr[1, t][None]) * l_scr[t][None]
        dk, dv = key_grads(p_far[:, t, :QT], dp_far[:, t, :QT], factor, d_scr[t], qs[t], dos[t], ds_1.at[t])
        if t == 0:
            acc[1, :, :WIDTH] = dk
            acc[1, :, WIDTH:] = dv
        else:
            acc[1, :, :WIDTH] += dk
            acc[1, :, WIDTH:] += dv

    def grads(role):
        return jnp.concatenate([acc[role, :, :WIDTH] * SCALE, acc[role, :, WIDTH:]], axis=1)

    g1_out[...] = grads(1).astype(jnp.bfloat16)
    trade = copy_to(g1_out, g1_in, send_g, recv_g, partner, head)
    trade.start()
    for t in range(TILES):
        f = t * QT
        factor = jnp.exp2(m_scr[1 + t :, t] - m_scr[1, t][None]) * l_scr[t][None]
        dk, dv = key_grads(
            p_far[t:, t, QT:], dp_far[t:, t, QT:], factor, d_scr[t], qs[t], dos[t], ds_2.at[t, pl.ds(f, ROWS - f)]
        )
        if t == 0:
            acc[2, :, :WIDTH] = dk
            acc[2, :, WIDTH:] = dv
        else:
            acc[2, f:, :WIDTH] += dk
            acc[2, f:, WIDTH:] += dv
    trade.wait_recv()
    none = jnp.zeros((ROWS, 2 * WIDTH), jnp.float32)
    traded = g1_in[...].astype(jnp.float32)
    prev_out[...] = (grads(2) + jnp.where(odd, traded, none)).astype(jnp.bfloat16)
    summed = []
    for s in range(1, n_head):
        x = lax.rem(head + s, n_head)
        some = pl.ds(pl.multiple_of(x * part + STRAIGHT, 16), part - STRAIGHT)
        cp = copy_to(prev_out.at[some], got_part.at[s - 1], send_part.at[s - 1], recv_part.at[s - 1], me, x)
        cp.start()
        summed.append(cp)
    back = []
    for s in range(n_head):
        x = lax.rem(head + s, n_head)
        some = pl.ds(pl.multiple_of(x * part, part), STRAIGHT)
        cp = copy_to(prev_out.at[some], got_z.at[s], send_z.at[s], recv_z.at[s], before, x)
        cp.start()
        back.append(cp)
    for t in reversed(range(TILES)):
        n = (t + 1) * QT
        factor = jnp.exp2(m_scr[0, t] - m_scr[1, t]) * l_scr[t]
        dk, dv = key_grads(
            p_own[t, :n], dp_own[t, :n], factor, d_scr[t], qs[t], dos[t], ds_0.at[t, pl.ds(0, n)]
        )
        if t == TILES - 1:
            acc[0, :, :WIDTH] = dk
            acc[0, :, WIDTH:] = dv
        else:
            acc[0, :n, :WIDTH] += dk
            acc[0, :n, WIDTH:] += dv
    acc[0] = grads(0) + jnp.where(odd, none, g1_in[...].astype(jnp.float32))
    own_out[...] = acc[0].astype(jnp.bfloat16)
    across = []
    for s in range(1, n_head):
        x = lax.rem(head + s, n_head)
        cp = copy_to(own_out.at[pl.ds(x * part, part)], got_x.at[s - 1], send_x.at[s - 1], recv_x.at[s - 1], me, x)
        cp.start()
        across.append(cp)
    for cp in summed:
        cp.wait_recv()
    some = pl.ds(pl.multiple_of(head * part + STRAIGHT, 16), part - STRAIGHT)
    rest = prev_out[some, :].astype(jnp.float32)
    for s in range(n_head - 1):
        rest = rest + got_part[s].astype(jnp.float32)
    rest_out[...] = rest.astype(jnp.bfloat16)
    cp = copy_to(rest_out, got_rest, send_rest, recv_rest, before, head)
    cp.start()
    back.append(cp)
    for t in range(TILES):
        n = (t + 1) * QT
        f = t * QT
        k1 = role_k[:, :QT].reshape(ROWS, WIDTH)
        k2 = role_k[t:, QT:].reshape(ROWS - f, WIDTH)
        dq = dot(kv[0, 0, :n], ds_0[t, :n], 0, 0) + dot(k1, ds_1[t], 0, 0) + dot(k2, ds_2[t, f:], 0, 0)
        dq = dq * SCALE
        rows = pl.ds(t * QT, QT)
        for h in range(HEADS):
            dq_out[rows, h * WIDTH : (h + 1) * WIDTH] = dq[:, h * QT : (h + 1) * QT].T.astype(dq_out.dtype)
    for cp in back:
        cp.wait_recv()
    came = got_z[0].astype(jnp.float32)
    for s in range(1, n_head):
        came = came + got_z[s].astype(jnp.float32)
    came = jnp.concatenate([came, got_rest[...].astype(jnp.float32)], axis=0)
    swap_out[...] = came.astype(jnp.bfloat16)
    swap = copy_to(swap_out, swap_in, send_s, recv_s, partner, head)
    swap.start()
    total = acc[0, pl.ds(head * part, part), :]
    for cp in across:
        cp.wait_recv()
    for s in range(n_head - 1):
        total = total + got_x[s].astype(jnp.float32)
    swap.wait_recv()
    straight = lax.rem(seq_ref[after], 2) == lax.rem(own, 2)
    total = total + jnp.where(straight, came, swap_in[...].astype(jnp.float32))
    dk_ref[...] = total[:, :WIDTH].astype(jnp.bfloat16)
    dv_ref[...] = total[:, WIDTH:].astype(jnp.bfloat16)
    for cp in list(far.values()) + near + list(forwards.values()) + [trade] + summed + back + across + [swap]:
        cp.wait_send()


def hand_on_kernel(dq_ref, dk_ref, dv_ref, dq_out, dk_out, dv_out, sem):
    copies = []
    for i, (src, dst) in enumerate(((dq_ref, dq_out), (dk_ref, dk_out), (dv_ref, dv_out))):
        cp = pltpu.make_async_copy(src, dst, sem.at[i])
        cp.start()
        copies.append(cp)
    for cp in copies:
        cp.wait()


def shards(queries, keys, values, out_grad, doc_start, block_seq):
    n_ctx = lax.axis_size("ctx")
    n_head = lax.axis_size("head")
    part = ROWS // n_head
    smem = pl.BlockSpec(memory_space=pltpu.SMEM)
    vmem = pl.BlockSpec(memory_space=pltpu.VMEM)
    hbm = pl.BlockSpec(memory_space=pltpu.HBM)
    f32 = jnp.float32
    bf16 = jnp.bfloat16
    dma = pltpu.SemaphoreType.DMA
    grads = pl.pallas_call(
        functools.partial(backward_kernel, n_ctx, n_head),
        out_shape=(
            pltpu.VMEM(queries.shape, bf16),
            pltpu.VMEM((part, WIDTH), bf16),
            pltpu.VMEM((part, WIDTH), bf16),
        ),
        in_specs=[smem, vmem, hbm, hbm, hbm, hbm],
        out_specs=(vmem, vmem, vmem),
        scratch_shapes=[
            pltpu.VMEM((TILES, COLS, WIDTH), bf16),
            pltpu.VMEM((TILES, COLS, WIDTH), bf16),
            pltpu.VMEM((4, 2, ROWS, WIDTH), bf16),
            pltpu.VMEM((CHUNKS, 2 * QT, WIDTH), bf16),
            pltpu.VMEM((CHUNKS, 2 * QT, WIDTH), bf16),
            pltpu.VMEM((3, ROWS, 2 * WIDTH), f32),
            pltpu.VMEM((TILES, ROWS, COLS), f32),
            pltpu.VMEM((TILES, ROWS, COLS), f32),
            pltpu.VMEM((CHUNKS, TILES, 2 * QT, COLS), f32),
            pltpu.VMEM((CHUNKS, TILES, 2 * QT, COLS), f32),
            pltpu.VMEM((TILES, ROWS, COLS), bf16),
            pltpu.VMEM((TILES, ROWS, COLS), bf16),
            pltpu.VMEM((TILES, ROWS, COLS), bf16),
            pltpu.VMEM((CHUNKS + 1, TILES, 1, COLS), f32),
            pltpu.VMEM((TILES, 1, COLS), f32),
            pltpu.VMEM((TILES, 1, COLS), f32),
            pltpu.VMEM((ROWS, 2 * WIDTH), bf16),
            pltpu.VMEM((ROWS, 2 * WIDTH), bf16),
            pltpu.VMEM((ROWS, 2 * WIDTH), bf16),
            pltpu.VMEM((ROWS, 2 * WIDTH), bf16),
            pltpu.VMEM((n_head, STRAIGHT, 2 * WIDTH), bf16),
            pltpu.VMEM((n_head - 1, part - STRAIGHT, 2 * WIDTH), bf16),
            pltpu.VMEM((part - STRAIGHT, 2 * WIDTH), bf16),
            pltpu.VMEM((part - STRAIGHT, 2 * WIDTH), bf16),
            pltpu.VMEM((n_head - 1, part, 2 * WIDTH), bf16),
            pltpu.VMEM((part, 2 * WIDTH), bf16),
            pltpu.VMEM((part, 2 * WIDTH), bf16),
            dma((2, HEADS)),
            dma((2,)),
            dma((2 * CHUNKS,)),
            dma((2 * CHUNKS,)),
            dma((2,)),
            dma((2,)),
            dma((2 * CHUNKS,)),
            dma((2 * CHUNKS,)),
            dma,
            dma,
            dma((n_head,)),
            dma((n_head,)),
            dma((n_head - 1,)),
            dma((n_head - 1,)),
            dma,
            dma,
            dma((n_head - 1,)),
            dma((n_head - 1,)),
            dma,
            dma,
        ],
        compiler_params=pltpu.CompilerParams(
            collective_id=0, has_side_effects=True, vmem_limit_bytes=VMEM_LIMIT
        ),
        name="backward",
    )(
        block_seq,
        doc_start.reshape(TILES, QT),
        queries.reshape(TILES, QT, HEADS * WIDTH),
        keys,
        values,
        out_grad.reshape(TILES, QT, HEADS * WIDTH),
    )
    return pl.pallas_call(
        hand_on_kernel,
        out_shape=tuple(jax.ShapeDtypeStruct(g.shape, g.dtype) for g in grads),
        in_specs=[vmem] * 3,
        out_specs=(hbm,) * 3,
        scratch_shapes=[dma((3,))],
        compiler_params=pltpu.CompilerParams(vmem_limit_bytes=1024 * 1024),
        name="hand_on",
    )(*grads)


def solution(mesh):
    return jax.shard_map(
        shards,
        mesh=mesh,
        in_specs=(
            P("ctx", "head"),
            P("ctx", None),
            P("ctx", None),
            P("ctx", "head"),
            P("ctx"),
            P(),
        ),
        out_specs=(P("ctx", "head"), P(("ctx", "head"), None), P(("ctx", "head"), None)),
        check_vma=False,
    )
```
